32 devices in a mesh: groups: 2 (over y), vox: 4 (over z), chan: 2 (over x), frm: 2 (over core).
Axes of the slice: x: 2, y: 2, z: 4, core: 2. Of those that a mesh axis runs over, the one named last changes fastest.
Arguments:
- echo_data: bfloat16 [8, 2, 1024, 2, 512], P(('groups', 'vox'), 'chan', None, None, 'frm'), parts along dimension 0, may hold values from -36 to 36
- tile_weights: bfloat16 [4, 2, 64, 128, 128], P('vox', 'chan'), may hold values from -0.0625 to 0.0625
- tile_target: int32 [4, 2, 64], P('vox', 'chan'), may hold values from 0 to 1
- tile_offset: int32 [4, 2, 64], P('vox', 'chan'), may hold values from 0 to 896
- tile_count: int32 [4, 2], P('vox', 'chan'), may hold values from 8 to 64, as said below
- grid_map: int32 [4, 256], P('vox'), may hold values from 0 to 255, each once within a row
- psf_kernel: float32 [5, 5], replicated, may hold values from -1.25 to 1.25
Outputs:
- psf_image: float32 [64, 32, 512], P(('groups', 'vox'), 'chan', 'frm'), parts along dimension 0
The draws below stay inside these ranges and needn't reach their ends.
There are 2 independent parts, one for each index of `groups`. The reference program is written for one: setup_inputs(seed, part) draws one part's arguments, and reference() takes and returns one part's arrays. A program takes and returns all parts, laid end to end along the dimension named above; an argument that names none is the same for every part. Nothing has to cross between parts.
Inputs may be any that keep to these rules, and one draw needn't show every extreme that they name: `tile_count`: in each voxel block exactly one channel group uses all 64 slots; the others use far fewer. `grid_map`: each block's row is a permutation of 0 to 255.
All inputs are finite; a program needn't handle non-finite values.
Results may differ from the reference program's by a relative error of at most 0.014.
Values may be sent and summed in bfloat16 or wider, within the bound.
No kernel may reach another device: no remote copies, remote signals or barrier semaphores. Data moves between devices by JAX's collectives and lax.ppermute only.
A program may use at most 64 MiB of HBM per device.

```python
import math
import jax
import jax.numpy as jnp
from jax import lax

FRAMES = 512
TILE = 128
VOX_DEV = 256
ROWS = 1024
TCAP = 64
BLOCKS = 4
CGROUPS = 2
NA = 32
NB = 32


def draw_echo_data(key, part):
    key_rows, key_frames, key_values = jax.random.split(jax.random.fold_in(key, 5), 3)
    shape_all = (BLOCKS, CGROUPS, ROWS, 2, FRAMES)
    row_scale = jnp.exp(jax.random.uniform(key_rows, (BLOCKS, CGROUPS, ROWS, 1, 1), jnp.float32, math.log(0.3), math.log(3.0)))
    frame_scale = jnp.exp(jax.random.uniform(key_frames, (FRAMES,), jnp.float32, 0.0, math.log(3.0)))
    values = jax.random.truncated_normal(key_values, -4.0, 4.0, shape_all, jnp.float32)
    return (values * row_scale * frame_scale).astype(jnp.bfloat16)


def draw_tile_count(key, part):
    key_busy, key_base = jax.random.split(jax.random.fold_in(key, 11))
    busiest = jax.random.randint(key_busy, (BLOCKS, 1), 0, CGROUPS)
    base_counts = jax.random.randint(key_base, (BLOCKS, CGROUPS), TCAP // 8, TCAP // 3 + 1)
    group_ids = jnp.arange(CGROUPS, dtype=jnp.int32)[None, :]
    return jnp.where(group_ids == busiest, TCAP, base_counts).astype(jnp.int32)


def plant(entries, key, least, high):
    extent = entries.shape
    spot = [jax.random.randint(jax.random.fold_in(key, axis), (), 0, extent[axis]) for axis in range(len(extent))]
    entries = entries.at[tuple(spot)].set(least)
    longest = extent.index(max(extent))
    spot[longest] = (spot[longest] + 1) % extent[longest]
    return entries.at[tuple(spot)].set(high)


def block_scale(stream_key, extent, cuts, least, largest):
    level, own = 1.0, jax.random.fold_in(stream_key, 6)
    for dim, parts in cuts:
        steps = jnp.exp(jax.random.uniform(jax.random.fold_in(own, dim), (parts,), jnp.float32, least / len(cuts), largest / len(cuts)))
        level = level * jnp.repeat(steps, extent[dim] // parts).reshape([-1 if axis == dim else 1 for axis in range(len(extent))])
    return level


def scatter_about(rng, dims, deviation, most, cuts=(), kind=jnp.bfloat16):
    result = deviation * jax.random.normal(rng, dims, jnp.float32)
    if cuts:
        result = result * block_scale(rng, dims, cuts, -0.22, 0.18)
    return jnp.clip(result, -most, most).astype(kind)


def setup_inputs(seed: int = 0, part: int = 0) -> dict:
    key_of = jax.random.split(jax.random.key(seed), 8)
    part_keys = jax.random.split(jax.random.fold_in(key_of[7], part), 8)
    return {
        "echo_data": draw_echo_data(jax.random.fold_in(jax.random.fold_in(key_of[7], part), 71), part),
        "tile_weights": scatter_about(key_of[1], (BLOCKS, CGROUPS, TCAP, TILE, TILE), (TILE * TCAP) ** -0.5, 0.0625, ((0, 4), (1, 2))),
        "tile_target": plant(jax.random.randint(key_of[2], (BLOCKS, CGROUPS, TCAP), 0, VOX_DEV // TILE), jax.random.fold_in(key_of[2], 1), 0, (VOX_DEV // TILE) - 1).astype(jnp.int32),
        "tile_offset": plant(jax.random.randint(key_of[3], (BLOCKS, CGROUPS, TCAP), 0, ROWS - TILE + 1), jax.random.fold_in(key_of[3], 1), 0, ROWS - TILE).astype(jnp.int32),
        "tile_count": draw_tile_count(jax.random.fold_in(key_of[7], 71), part),
        "grid_map": jax.vmap(lambda own: jax.random.permutation(own, VOX_DEV))(jax.random.split(key_of[5], BLOCKS)).reshape((BLOCKS, VOX_DEV)).astype(jnp.int32),
        "psf_kernel": scatter_about(key_of[6], (5, 5), 25 ** -0.5, 1.25, (), jnp.float32),
    }


POLY_COEFFS = (1.0, -0.6, 0.15, -0.03)

def complex_times(left_real, left_imag, right_real, right_imag):
    level = lax.Precision.HIGH
    real_part = jnp.dot(left_real, right_real, precision=level, preferred_element_type=jnp.float32) - jnp.dot(left_imag, right_imag, precision=level, preferred_element_type=jnp.float32)
    imag_part = jnp.dot(left_real, right_imag, precision=level, preferred_element_type=jnp.float32) + jnp.dot(left_imag, right_real, precision=level, preferred_element_type=jnp.float32)
    return (real_part, imag_part)

def beam_block(block_items):
    echo_block, weight_block, target_block, offset_block, count_block = block_items
    group_total = echo_block.shape[0]
    flat_echo = echo_block.reshape(group_total, ROWS, 2 * FRAMES)
    slot_total = group_total * TCAP
    slot_ids = jnp.arange(slot_total, dtype=jnp.int32)
    group_ids = slot_ids // TCAP
    keep_slots = slot_ids % TCAP < count_block[group_ids]
    zero_index = jnp.zeros((), jnp.int32)

    def add_tile(totals, item):
        weight_tile, group_id, target_id, offset_id, keep_tile = item
        samples = lax.dynamic_slice(flat_echo, (group_id, offset_id, zero_index), (1, TILE, 2 * FRAMES))[0]
        product = jnp.dot(weight_tile, samples, preferred_element_type=jnp.float32)
        product = jnp.where(keep_tile, product, jnp.zeros_like(product))
        return (totals.at[target_id].add(product), None)
    start_totals = jnp.zeros((VOX_DEV // TILE, TILE, 2 * FRAMES), jnp.float32)
    items = (weight_block.reshape(slot_total, TILE, TILE), group_ids, target_block.reshape(slot_total), offset_block.reshape(slot_total), keep_slots)
    totals, unused = lax.scan(add_tile, start_totals, items)
    return totals.reshape(VOX_DEV, 2, FRAMES)

def reference(echo_data, tile_weights, tile_target, tile_offset, tile_count, grid_map, psf_kernel):
    beams = lax.map(beam_block, (echo_data, tile_weights, tile_target, tile_offset, tile_count))
    arranged = jax.vmap(lambda beam_rows, order_ids: beam_rows[order_ids])(beams, grid_map)
    beamformed = arranged.reshape(NA, NB, 2, FRAMES).astype(jnp.bfloat16)
    stacked = beamformed.reshape(NA * NB, 2 * FRAMES)
    gram_block = lax.dot_general(stacked, stacked, (((0,), (0,)), ((), ())), preferred_element_type=jnp.float32)
    gram_real = gram_block[:FRAMES, :FRAMES] + gram_block[FRAMES:, FRAMES:]
    gram_imag = gram_block[:FRAMES, FRAMES:] - gram_block[FRAMES:, :FRAMES]
    factor = FRAMES / jnp.trace(gram_real)
    norm_real = factor * gram_real
    norm_imag = factor * gram_imag
    echo_real = beamformed[:, :, 0, :].reshape(NA * NB, FRAMES).astype(jnp.float32)
    echo_imag = beamformed[:, :, 1, :].reshape(NA * NB, FRAMES).astype(jnp.float32)
    term_real = POLY_COEFFS[3] * echo_real
    term_imag = POLY_COEFFS[3] * echo_imag
    for degree in (2, 1, 0):
        term_real, term_imag = complex_times(term_real, term_imag, norm_real, norm_imag)
        term_real = term_real + POLY_COEFFS[degree] * echo_real
        term_imag = term_imag + POLY_COEFFS[degree] * echo_imag
    envelope = jnp.sqrt(term_real * term_real + term_imag * term_imag + 1e-06)
    envelope = envelope.reshape(NA, NB, FRAMES)
    padded = jnp.pad(envelope, ((2, 2), (2, 2), (0, 0)))
    psf_image = jnp.zeros_like(envelope)
    for shift_a in range(5):
        for shift_b in range(5):
            psf_image = psf_image + psf_kernel[shift_a, shift_b] * padded[shift_a:shift_a + NA, shift_b:shift_b + NB]
    return psf_image
```

```python
import functools

import jax
import jax.numpy as jnp
from jax import lax
from jax.experimental import pallas as pl
from jax.experimental.pallas import tpu as pltpu
from jax.sharding import PartitionSpec as P

POLY_COEFFS = (1.0, -0.6, 0.15, -0.03)
HALO = 2
BATCH = 4
EDGE = 4
VMEM_LIMIT = 56 * 2**20
F32 = jnp.float32
BF16 = jnp.bfloat16


def split(x):
    high = x.astype(BF16)
    return high, (x - high.astype(F32)).astype(BF16)


def dot(a, b, dims=((1,), (0,))):
    return lax.dot_general(a, b, (dims, ((), ())), preferred_element_type=F32)


def das_kernel(
    count, target, offset, echo, weights, grid_map, own_out, send_out, dense, arranged, *, chans, lat
):
    slots, tile = weights.shape[0], weights.shape[1]
    voxels = grid_map.shape[1]
    tiles_out = voxels // tile
    spans = echo.shape[0] // tile
    live = count[0]
    dense[...] = jnp.zeros_like(dense)
    lanes = lax.broadcasted_iota(jnp.int32, (tile, tile), 1)

    def one_batch(turn, carry):
        for lane in range(BATCH):
            at = turn * BATCH + lane
            slot = jnp.minimum(at, slots - 1)
            goal = jnp.where(at < live, target[slot], tiles_out)
            first = offset[slot]
            span, shift = first // tile, first % tile
            turned = pltpu.roll(weights[slot].astype(F32), shift, 1)
            dense[goal, span] += jnp.where(lanes >= shift, turned, 0.0)
            dense[goal, span + 1] += jnp.where(lanes < shift, turned, 0.0)
        return carry

    lax.fori_loop(0, (live + BATCH - 1) // BATCH, one_batch, 0)

    rows = []
    for t in range(tiles_out):
        rows.append(jnp.concatenate([dense[t, s] for s in range(spans)], axis=1))
    high, low = split(jnp.concatenate(rows, axis=0))
    data = echo[...]
    sums = dot(high, data) + dot(low, data)
    voxel_ids = lax.broadcasted_iota(jnp.int32, (voxels, voxels), 0)
    placing = (voxel_ids == grid_map[...]).astype(F32).astype(BF16)
    high, low = split(sums)
    arranged[...] = dot(placing, high, ((0,), (0,))) + dot(placing, low, ((0,), (0,)))
    depth = voxels // lat
    width = depth // chans
    mine = lax.axis_index("chan")
    for a in range(lat):
        for step in range(chans):
            first = pl.multiple_of(a * depth + (mine ^ step) * width, 8)
            rows = arranged[pl.ds(first, width), :]
            if step == 0:
                own_out[a * width : (a + 1) * width, :] = rows
            else:
                send_out[step - 1, a * width : (a + 1) * width, :] = rows.astype(BF16)


def gram_parts(a, b):
    con = ((0,), (0,))
    return [dot(a, a, con), dot(a, b, con), dot(b, b, con)]


def gram_kernel(*refs):
    out = refs[-1]
    count = (len(refs) - 1) // 2
    a = jnp.concatenate([r[...] for r in refs[:count]], axis=0)
    b = jnp.concatenate([r[...] for r in refs[count : 2 * count]], axis=0)
    for i, t in enumerate(gram_parts(a, b)):
        out[i] = t


def filter_kernel(psf, gram, *refs, fresh, inner, chans, lat, width, vox_total, frames):
    total_blocks = (len(refs) - 5) // 2
    mine = refs[:total_blocks]
    other = refs[total_blocks : 2 * total_blocks]
    out, stack_a, stack_b, mat_high, mat_low = refs[2 * total_blocks :]
    n = lat * width
    half = mine[0].shape[1]
    hf = half // 2
    vox = lax.axis_index("vox")
    chan = lax.axis_index("chan")
    for i in range(total_blocks):
        stack_a[i] = mine[i][...]
        stack_b[i] = other[i][...]
    parts = [gram[i] for i in range(3)]
    if fresh:
        first = total_blocks - fresh
        a = stack_a[first:].reshape(fresh * n, half)
        b = stack_b[first:].reshape(fresh * n, half)
        parts = [p + t for p, t in zip(parts, gram_parts(a, b))]

    def diag_sum(t):
        r = lax.broadcasted_iota(jnp.int32, t.shape, 0)
        c = lax.broadcasted_iota(jnp.int32, t.shape, 1)
        return jnp.sum(jnp.where(r == c, t, 0.0))

    factor = frames / (diag_sum(parts[0]) + diag_sum(parts[2]))
    for i, t in enumerate(parts):
        real = factor * (t[:hf, :hf] + t[hf:, hf:])
        imag = factor * (t[:hf, hf:] - t[hf:, :hf])
        real_high, real_low = split(real)
        imag_high, imag_low = split(imag)
        for ref, re, im in ((mat_high, real_high, imag_high), (mat_low, real_low, imag_low)):
            ref[i, :hf, :hf] = re
            ref[i, hf:, hf:] = re
            ref[i, :hf, hf:] = im
            ref[i, hf:, :hf] = -im

    def place(v):
        away = vox ^ v
        return jnp.where(away >= inner // 2, inner // 2 + (away ^ (inner - 1)), away)

    edge = HALO * width
    if vox_total > inner:
        above, below = inner * chans, (inner + 1) * chans
    else:
        above = place(jnp.maximum(vox - 1, 0)) * chans
        below = place(jnp.minimum(vox + 1, vox_total - 1)) * chans

    def column(stack, away):
        return jnp.concatenate(
            [
                stack[above + away, n - edge :, :],
                stack[away],
                stack[below + away, :edge, :],
            ],
            axis=0,
        )

    rows = (lat + 2 * HALO) * width
    lat_all = lat + 2 * HALO
    pr = lax.broadcasted_iota(jnp.int32, (lat_all * EDGE, rows), 0)
    pc = lax.broadcasted_iota(jnp.int32, (lat_all * EDGE, rows), 1)
    x_rows = [[column(stack_a, 0)], [column(stack_b, 0)]]
    sides = [-1, 1] if chans > 2 else [0]
    side_start = []
    for side in sides:
        if side == 0:
            away = 1
            start = jnp.where(chan == 0, 0, width - EDGE)
            base = jnp.where(chan == 0, width, 0) + start
        else:
            near = jnp.clip(chan + side, 0, chans - 1)
            away = chan ^ near
            start = 0 if side == 1 else width - EDGE
            base = near * width + start
            base = jnp.where(near == chan, -(10**6), base)
        pick = ((pr // EDGE == pc // width) & (pc % width == start + pr % EDGE)).astype(F32).astype(BF16)
        for which, stack in enumerate((stack_a, stack_b)):
            x_rows[which].append(dot(pick, column(stack, away)).astype(BF16))
        side_start.append(base)
    xa, xb = (jnp.concatenate(x, axis=0) for x in x_rows)

    def times(za, zb, last):
        m = [(mat_high[i], mat_low[i]) for i in range(3)]
        (ah, al), (bh, bl) = split(za), split(zb)
        back = ((1,), (1,))

        def product(h, l, mat, dims):
            return dot(h, mat[0], dims) + dot(l, mat[0], dims) + dot(h, mat[1], dims)

        fwd = ((1,), (0,))
        new_a = product(ah, al, m[0], fwd) + product(bh, bl, m[1], back)
        if last:
            return new_a, None
        return new_a, product(ah, al, m[1], fwd) + product(bh, bl, m[2], fwd)

    fa, fb = xa.astype(F32), xb.astype(F32)
    za, zb = POLY_COEFFS[3] * fa, POLY_COEFFS[3] * fb
    for degree in (2, 1, 0):
        za, zb = times(za, zb, degree == 0)
        za = za + POLY_COEFFS[degree] * fa
        if degree:
            zb = zb + POLY_COEFFS[degree] * fb
    env = jnp.sqrt(za[:, :hf] * za[:, :hf] + za[:, hf:] * za[:, hf:] + 1e-06)

    total = env.shape[0]
    outs = lax.broadcasted_iota(jnp.int32, (n, total), 0)
    ins = lax.broadcasted_iota(jnp.int32, (n, total), 1)
    lat_in = ins // width
    dep_in = chan * width + ins % width
    for s, base in enumerate(side_start):
        local = ins - rows - s * lat_all * EDGE
        here = local >= 0
        lat_in = jnp.where(here, local // EDGE, lat_in)
        dep_in = jnp.where(here, base + local % EDGE, dep_in)
    tap_a = lat_in - outs // width
    tap_b = dep_in - (chan * width + outs % width) + HALO
    lat_grid = vox * lat + lat_in - HALO
    inside = (lat_grid >= 0) & (lat_grid < vox_total * lat)
    tap = jnp.where(
        inside & (tap_a >= 0) & (tap_a < 5) & (tap_b >= 0) & (tap_b < 5), tap_a * 5 + tap_b, -1
    )
    mix = jnp.zeros((n, total), F32)
    for i in range(5):
        for j in range(5):
            mix = jnp.where(tap == i * 5 + j, psf[i, j], mix)
    mh, ml = split(mix)
    eh, el = split(env)
    out[...] = dot(mh, eh) + dot(ml, eh) + dot(mh, el)


def shards(mesh, echo_data, tile_weights, tile_target, tile_offset, tile_count, grid_map, psf_kernel):
    rows, hf = echo_data.shape[2], echo_data.shape[4]
    slots, tile = tile_weights.shape[2], tile_weights.shape[3]
    voxels = grid_map.shape[1]
    chans, vox_total, frms = mesh.shape["chan"], mesh.shape["vox"], mesh.shape["frm"]
    lat = 8
    width = voxels // lat // chans
    n = lat * width
    smem = pl.BlockSpec(memory_space=pltpu.SMEM)
    vmem = pl.BlockSpec(memory_space=pltpu.VMEM)
    echo = echo_data.reshape(rows, 2 * hf)
    own, sent = pl.pallas_call(
        functools.partial(das_kernel, chans=chans, lat=lat),
        out_shape=(
            jax.ShapeDtypeStruct((n, 2 * hf), F32),
            jax.ShapeDtypeStruct((chans - 1, n, 2 * hf), BF16),
        ),
        in_specs=[smem, smem, smem, vmem, vmem, vmem],
        out_specs=(vmem, vmem),
        scratch_shapes=[
            pltpu.VMEM((voxels // tile + 1, rows // tile + 1, tile, tile), F32),
            pltpu.VMEM((voxels, 2 * hf), F32),
        ],
        compiler_params=pltpu.CompilerParams(vmem_limit_bytes=VMEM_LIMIT),
    )(
        tile_count.reshape(-1),
        tile_target.reshape(-1),
        tile_offset.reshape(-1),
        echo,
        tile_weights.reshape(slots, tile, tile),
        grid_map,
    )
    inner = min(vox_total, 4)

    def peer(x, dv, dc):
        pairs = [
            (v * chans + c, (v ^ dv) * chans + (c ^ dc))
            for v in range(vox_total)
            for c in range(chans)
        ]
        return lax.ppermute(x, ("vox", "chan"), pairs)

    for step in range(1, chans):
        own = own + peer(sent[step - 1], 0, step).astype(F32)
    own = own.astype(BF16)
    crossed = peer(own, inner - 1, 0)
    near = [(dv, dc) for dv in range(inner // 2) for dc in range(chans)]
    mine = [own] + [peer(own, dv, dc) for dv, dc in near[1:]]
    mine += [crossed] + [peer(crossed, dv, dc) for dv, dc in near[1:]]

    def to_other(x):
        return lax.ppermute(x, "frm", [(f, f ^ 1) for f in range(frms)])

    other = [to_other(x) for x in mine]
    groups = inner * chans
    part = groups // 2

    def gram_of(a, b):
        cost = pl.CostEstimate(
            flops=6 * len(a) * n * (2 * hf) ** 2, bytes_accessed=12 * (2 * hf) ** 2, transcendentals=0
        )
        return pl.pallas_call(
            gram_kernel,
            out_shape=jax.ShapeDtypeStruct((3, 2 * hf, 2 * hf), F32),
            in_specs=[vmem] * (2 * len(a)),
            out_specs=vmem,
            cost_estimate=cost,
            compiler_params=pltpu.CompilerParams(vmem_limit_bytes=VMEM_LIMIT),
        )(*a, *b)

    gram = gram_of(mine[:part], other[:part])
    fresh = groups - part
    if vox_total > inner:
        gram = gram + gram_of(mine[part:], other[part:])
        fresh = 0
        away = inner
        while away < vox_total:
            gram = gram + peer(gram, away, 0)
            away *= 2
        for go in (1, -1):
            pairs = [(v, v + go) for v in range(vox_total) if 0 <= v + go < vox_total]
            mine += [lax.ppermute(x, "vox", pairs) for x in mine[:chans]]
            other += [lax.ppermute(x, "vox", pairs) for x in other[:chans]]
    blocks = len(mine)
    out = pl.pallas_call(
        functools.partial(
            filter_kernel,
            fresh=fresh,
            inner=inner,
            chans=chans,
            lat=lat,
            width=width,
            vox_total=vox_total,
            frames=float(frms * hf),
        ),
        out_shape=jax.ShapeDtypeStruct((n, hf), F32),
        in_specs=[smem, vmem] + [vmem] * (2 * blocks),
        out_specs=vmem,
        scratch_shapes=[
            pltpu.VMEM((blocks, n, 2 * hf), BF16),
            pltpu.VMEM((blocks, n, 2 * hf), BF16),
            pltpu.VMEM((3, 2 * hf, 2 * hf), BF16),
            pltpu.VMEM((3, 2 * hf, 2 * hf), BF16),
        ],
        compiler_params=pltpu.CompilerParams(vmem_limit_bytes=VMEM_LIMIT),
    )(psf_kernel, gram, *mine, *other)
    return out.reshape(lat, width, hf)


def solution(mesh):
    in_specs = (
        P(("groups", "vox"), "chan", None, None, "frm"),
        P("vox", "chan", None, None, None),
        P("vox", "chan", None),
        P("vox", "chan", None),
        P("vox", "chan"),
        P("vox", None),
        P(),
    )
    out_specs = P(("groups", "vox"), "chan", "frm")
    return jax.shard_map(
        functools.partial(shards, mesh),
        mesh=mesh,
        in_specs=in_specs,
        out_specs=out_specs,
        check_vma=False,
    )
```

```python
import functools

import jax
import jax.numpy as jnp
from jax import lax
from jax.experimental import pallas as pl
from jax.experimental.pallas import tpu as pltpu
from jax.sharding import PartitionSpec as P

POLY_COEFFS = (1.0, -0.6, 0.15, -0.03)
HALO = 2
BATCH = 4
CHUNKS = 4
EDGE = 4
VMEM_LIMIT = 24 * 2**20
F32 = jnp.float32
BF16 = jnp.bfloat16


def split(x):
    high = x.astype(BF16)
    return high, (x - high.astype(F32)).astype(BF16)


def dot(a, b, dims=((1,), (0,))):
    return lax.dot_general(a, b, (dims, ((), ())), preferred_element_type=F32)


def das_kernel(
    count,
    target,
    offset,
    echo_hbm,
    weights_hbm,
    grid_map,
    own_out,
    send_out,
    echo,
    weights,
    dense,
    arranged,
    sems,
    *,
    chans,
    lat,
):
    slots, tile = weights.shape[0], weights.shape[1]
    chunk = slots // CHUNKS
    copies = [
        pltpu.make_async_copy(
            weights_hbm.at[pl.ds(i * chunk, chunk)], weights.at[pl.ds(i * chunk, chunk)], sems.at[i]
        )
        for i in range(CHUNKS)
    ]
    copies.append(pltpu.make_async_copy(echo_hbm, echo, sems.at[CHUNKS]))
    for copy in copies:
        copy.start()
    voxels = grid_map.shape[1]
    tiles_out = voxels // tile
    spans = echo.shape[0] // tile
    live = count[0]
    dense[...] = jnp.zeros_like(dense)
    lanes = lax.broadcasted_iota(jnp.int32, (tile, tile), 1)

    def one_batch(turn, carry):
        for lane in range(BATCH):
            at = turn * BATCH + lane
            slot = jnp.minimum(at, slots - 1)
            goal = jnp.where(at < live, target[slot], tiles_out)
            first = offset[slot]
            span, shift = first // tile, first % tile
            turned = pltpu.roll(weights[slot].astype(F32), shift, 1)
            dense[goal, span] += jnp.where(lanes >= shift, turned, 0.0)
            dense[goal, span + 1] += jnp.where(lanes < shift, turned, 0.0)
        return carry

    turns = (live + BATCH - 1) // BATCH
    for i in range(CHUNKS):
        copies[i].wait()
        last = jnp.minimum(turns, (i + 1) * chunk // BATCH)
        lax.fori_loop(i * chunk // BATCH, last, one_batch, 0)
    copies[CHUNKS].wait()

    rows = []
    for t in range(tiles_out):
        rows.append(jnp.concatenate([dense[t, s] for s in range(spans)], axis=1))
    high, low = split(jnp.concatenate(rows, axis=0))
    data = echo[...].reshape(echo.shape[0], 2 * echo.shape[2])
    sums = dot(high, data) + dot(low, data)
    voxel_ids = lax.broadcasted_iota(jnp.int32, (voxels, voxels), 0)
    placing = (voxel_ids == grid_map[...]).astype(F32).astype(BF16)
    high, low = split(sums)
    arranged[...] = dot(placing, high, ((0,), (0,))) + dot(placing, low, ((0,), (0,)))
    depth = voxels // lat
    width = depth // chans
    mine = lax.axis_index("chan")
    for a in range(lat):
        for step in range(chans):
            first = pl.multiple_of(a * depth + (mine ^ step) * width, 8)
            rows = arranged[pl.ds(first, width), :]
            if step == 0:
                own_out[a * width : (a + 1) * width, :] = rows
            else:
                send_out[step - 1, a * width : (a + 1) * width, :] = rows.astype(BF16)


def gram_parts(a, b):
    con = ((0,), (0,))
    return [dot(a, a, con), dot(a, b, con), dot(b, b, con)]


def gram_kernel(*refs):
    out = refs[-1]
    count = (len(refs) - 1) // 2
    a = jnp.concatenate([r[...] for r in refs[:count]], axis=0)
    b = jnp.concatenate([r[...] for r in refs[count : 2 * count]], axis=0)
    for i, t in enumerate(gram_parts(a, b)):
        out[i] = t


def filter_kernel(psf, gram, *refs, fresh, inner, chans, lat, width, vox_total, frames):
    total_blocks = (len(refs) - 5) // 2
    mine = refs[:total_blocks]
    other = refs[total_blocks : 2 * total_blocks]
    out, stack_a, stack_b, mat_high, mat_low = refs[2 * total_blocks :]
    n = lat * width
    half = mine[0].shape[1]
    hf = half // 2
    vox = lax.axis_index("vox")
    chan = lax.axis_index("chan")
    for i in range(total_blocks):
        stack_a[i] = mine[i][...]
        stack_b[i] = other[i][...]
    parts = [gram[i] for i in range(3)]
    if fresh:
        first = total_blocks - fresh
        a = stack_a[first:].reshape(fresh * n, half)
        b = stack_b[first:].reshape(fresh * n, half)
        parts = [p + t for p, t in zip(parts, gram_parts(a, b))]

    def diag_sum(t):
        r = lax.broadcasted_iota(jnp.int32, t.shape, 0)
        c = lax.broadcasted_iota(jnp.int32, t.shape, 1)
        return jnp.sum(jnp.where(r == c, t, 0.0))

    factor = frames / (diag_sum(parts[0]) + diag_sum(parts[2]))
    for i, t in enumerate(parts):
        real = factor * (t[:hf, :hf] + t[hf:, hf:])
        imag = factor * (t[:hf, hf:] - t[hf:, :hf])
        real_high, real_low = split(real)
        imag_high, imag_low = split(imag)
        for ref, re, im in ((mat_high, real_high, imag_high), (mat_low, real_low, imag_low)):
            ref[i, :hf, :hf] = re
            ref[i, hf:, hf:] = re
            ref[i, :hf, hf:] = im
            ref[i, hf:, :hf] = -im

    def place(v):
        away = vox ^ v
        return jnp.where(away >= inner // 2, inner // 2 + (away ^ (inner - 1)), away)

    edge = HALO * width
    if vox_total > inner:
        above, below = inner * chans, (inner + 1) * chans
    else:
        above = place(jnp.maximum(vox - 1, 0)) * chans
        below = place(jnp.minimum(vox + 1, vox_total - 1)) * chans

    def column(stack, away):
        return jnp.concatenate(
            [
                stack[above + away, n - edge :, :],
                stack[away],
                stack[below + away, :edge, :],
            ],
            axis=0,
        )

    rows = (lat + 2 * HALO) * width
    lat_all = lat + 2 * HALO
    pr = lax.broadcasted_iota(jnp.int32, (lat_all * EDGE, rows), 0)
    pc = lax.broadcasted_iota(jnp.int32, (lat_all * EDGE, rows), 1)
    x_rows = [[column(stack_a, 0)], [column(stack_b, 0)]]
    sides = [-1, 1] if chans > 2 else [0]
    side_start = []
    for side in sides:
        if side == 0:
            away = 1
            start = jnp.where(chan == 0, 0, width - EDGE)
            base = jnp.where(chan == 0, width, 0) + start
        else:
            near = jnp.clip(chan + side, 0, chans - 1)
            away = chan ^ near
            start = 0 if side == 1 else width - EDGE
            base = near * width + start
            base = jnp.where(near == chan, -(10**6), base)
        pick = ((pr // EDGE == pc // width) & (pc % width == start + pr % EDGE)).astype(F32).astype(BF16)
        for which, stack in enumerate((stack_a, stack_b)):
            x_rows[which].append(dot(pick, column(stack, away)).astype(BF16))
        side_start.append(base)
    xa, xb = (jnp.concatenate(x, axis=0) for x in x_rows)

    def times(za, zb, last):
        m = [(mat_high[i], mat_low[i]) for i in range(3)]
        (ah, al), (bh, bl) = split(za), split(zb)
        back = ((1,), (1,))

        def product(h, l, mat, dims):
            return dot(h, mat[0], dims) + dot(l, mat[0], dims) + dot(h, mat[1], dims)

        fwd = ((1,), (0,))
        new_a = product(ah, al, m[0], fwd) + product(bh, bl, m[1], back)
        if last:
            return new_a, None
        return new_a, product(ah, al, m[1], fwd) + product(bh, bl, m[2], fwd)

    fa, fb = xa.astype(F32), xb.astype(F32)
    za, zb = POLY_COEFFS[3] * fa, POLY_COEFFS[3] * fb
    for degree in (2, 1, 0):
        za, zb = times(za, zb, degree == 0)
        za = za + POLY_COEFFS[degree] * fa
        if degree:
            zb = zb + POLY_COEFFS[degree] * fb
    env = jnp.sqrt(za[:, :hf] * za[:, :hf] + za[:, hf:] * za[:, hf:] + 1e-06)

    total = env.shape[0]
    outs = lax.broadcasted_iota(jnp.int32, (n, total), 0)
    ins = lax.broadcasted_iota(jnp.int32, (n, total), 1)
    lat_in = ins // width
    dep_in = chan * width + ins % width
    for s, base in enumerate(side_start):
        local = ins - rows - s * lat_all * EDGE
        here = local >= 0
        lat_in = jnp.where(here, local // EDGE, lat_in)
        dep_in = jnp.where(here, base + local % EDGE, dep_in)
    tap_a = lat_in - outs // width
    tap_b = dep_in - (chan * width + outs % width) + HALO
    lat_grid = vox * lat + lat_in - HALO
    inside = (lat_grid >= 0) & (lat_grid < vox_total * lat)
    tap = jnp.where(
        inside & (tap_a >= 0) & (tap_a < 5) & (tap_b >= 0) & (tap_b < 5), tap_a * 5 + tap_b, -1
    )
    mix = jnp.zeros((n, total), F32)
    for i in range(5):
        for j in range(5):
            mix = jnp.where(tap == i * 5 + j, psf[i, j], mix)
    mh, ml = split(mix)
    eh, el = split(env)
    out[...] = dot(mh, eh) + dot(ml, eh) + dot(mh, el)


def shards(mesh, echo_data, tile_weights, tile_target, tile_offset, tile_count, grid_map, psf_kernel):
    rows, hf = echo_data.shape[2], echo_data.shape[4]
    slots, tile = tile_weights.shape[2], tile_weights.shape[3]
    voxels = grid_map.shape[1]
    chans, vox_total, frms = mesh.shape["chan"], mesh.shape["vox"], mesh.shape["frm"]
    lat = 8
    width = voxels // lat // chans
    n = lat * width
    smem = pl.BlockSpec(memory_space=pltpu.SMEM)
    vmem = pl.BlockSpec(memory_space=pltpu.VMEM)
    hbm = pl.BlockSpec(memory_space=pl.ANY)
    echo = echo_data.reshape(rows, 2, hf)
    own, sent = pl.pallas_call(
        functools.partial(das_kernel, chans=chans, lat=lat),
        out_shape=(
            pltpu.VMEM((n, 2 * hf), F32),
            pltpu.VMEM((chans - 1, n, 2 * hf), BF16),
        ),
        in_specs=[smem, smem, smem, hbm, hbm, vmem],
        out_specs=(vmem, vmem),
        scratch_shapes=[
            pltpu.VMEM((rows, 2, hf), BF16),
            pltpu.VMEM((slots, tile, tile), BF16),
            pltpu.VMEM((voxels // tile + 1, rows // tile + 1, tile, tile), F32),
            pltpu.VMEM((voxels, 2 * hf), F32),
            pltpu.SemaphoreType.DMA((CHUNKS + 1,)),
        ],
        compiler_params=pltpu.CompilerParams(vmem_limit_bytes=56 * 2**20),
    )(
        tile_count.reshape(-1),
        tile_target.reshape(-1),
        tile_offset.reshape(-1),
        echo,
        tile_weights.reshape(slots, tile, tile),
        grid_map,
    )
    inner = min(vox_total, 4)

    def peer(x, dv, dc):
        pairs = [
            (v * chans + c, (v ^ dv) * chans + (c ^ dc))
            for v in range(vox_total)
            for c in range(chans)
        ]
        return lax.ppermute(x, ("vox", "chan"), pairs)

    for step in range(1, chans):
        own = own + peer(sent[step - 1], 0, step).astype(F32)
    own = own.astype(BF16)
    crossed = peer(own, inner - 1, 0)
    near = [(dv, dc) for dv in range(inner // 2) for dc in range(chans)]
    mine = [own] + [peer(own, dv, dc) for dv, dc in near[1:]]
    mine += [crossed] + [peer(crossed, dv, dc) for dv, dc in near[1:]]

    def to_other(x):
        return lax.ppermute(x, "frm", [(f, f ^ 1) for f in range(frms)])

    groups = inner * chans
    part = groups // 2
    other = [to_other(x) for x in mine]

    def gram_of(a, b):
        cost = pl.CostEstimate(
            flops=60 * len(a) * n * (2 * hf) ** 2, bytes_accessed=12 * (2 * hf) ** 2, transcendentals=0
        )
        return pl.pallas_call(
            gram_kernel,
            out_shape=jax.ShapeDtypeStruct((3, 2 * hf, 2 * hf), F32),
            in_specs=[vmem] * (2 * len(a)),
            out_specs=vmem,
            cost_estimate=cost,
            compiler_params=pltpu.CompilerParams(vmem_limit_bytes=VMEM_LIMIT),
        )(*a, *b)

    gram = gram_of(mine[:part], other[:part])
    fresh = groups - part
    if vox_total > inner:
        gram = gram + gram_of(mine[part:], other[part:])
        fresh = 0
        away = inner
        while away < vox_total:
            gram = gram + peer(gram, away, 0)
            away *= 2
        for go in (1, -1):
            pairs = [(v, v + go) for v in range(vox_total) if 0 <= v + go < vox_total]
            mine += [lax.ppermute(x, "vox", pairs) for x in mine[:chans]]
            other += [lax.ppermute(x, "vox", pairs) for x in other[:chans]]
    blocks = len(mine)
    out = pl.pallas_call(
        functools.partial(
            filter_kernel,
            fresh=fresh,
            inner=inner,
            chans=chans,
            lat=lat,
            width=width,
            vox_total=vox_total,
            frames=float(frms * hf),
        ),
        out_shape=jax.ShapeDtypeStruct((n, hf), F32),
        in_specs=[smem, vmem] + [vmem] * (2 * blocks),
        out_specs=vmem,
        scratch_shapes=[
            pltpu.VMEM((blocks, n, 2 * hf), BF16),
            pltpu.VMEM((blocks, n, 2 * hf), BF16),
            pltpu.VMEM((3, 2 * hf, 2 * hf), BF16),
            pltpu.VMEM((3, 2 * hf, 2 * hf), BF16),
        ],
        compiler_params=pltpu.CompilerParams(vmem_limit_bytes=VMEM_LIMIT),
    )(psf_kernel, gram, *mine, *other)
    return out.reshape(lat, width, hf)


def solution(mesh):
    in_specs = (
        P(("groups", "vox"), "chan", None, None, "frm"),
        P("vox", "chan", None, None, None),
        P("vox", "chan", None),
        P("vox", "chan", None),
        P("vox", "chan"),
        P("vox", None),
        P(),
    )
    out_specs = P(("groups", "vox"), "chan", "frm")
    return jax.shard_map(
        functools.partial(shards, mesh),
        mesh=mesh,
        in_specs=in_specs,
        out_specs=out_specs,
        check_vma=False,
    )
```

```python
import functools

import jax
import jax.numpy as jnp
from jax import lax
from jax.experimental import pallas as pl
from jax.experimental.pallas import tpu as pltpu
from jax.sharding import PartitionSpec as P

POLY_COEFFS = (1.0, -0.6, 0.15, -0.03)
HALO = 2
BATCH = 4
CHUNKS = 4
EDGE = 2
DIAG = 128
OUTSIDE = -(10**6)
VMEM_LIMIT = 24 * 2**20
F32 = jnp.float32
BF16 = jnp.bfloat16


def split(x):
    high = x.astype(BF16)
    return high, (x - high.astype(F32)).astype(BF16)


def dot(a, b, dims=((1,), (0,))):
    return lax.dot_general(a, b, (dims, ((), ())), preferred_element_type=F32)


def das_kernel(
    count,
    target,
    offset,
    echo_hbm,
    weights_hbm,
    grid_map,
    psf,
    own_out,
    send_out,
    mix_out,
    echo,
    weights,
    dense,
    arranged,
    sems,
    *,
    chans,
    lat,
    vox_total,
):
    slots, tile = weights.shape[0], weights.shape[1]
    chunk = slots // CHUNKS
    copies = [
        pltpu.make_async_copy(
            weights_hbm.at[pl.ds(i * chunk, chunk)], weights.at[pl.ds(i * chunk, chunk)], sems.at[i]
        )
        for i in range(CHUNKS)
    ]
    copies.append(pltpu.make_async_copy(echo_hbm, echo, sems.at[CHUNKS]))
    for copy in copies:
        copy.start()
    voxels = grid_map.shape[1]
    tiles_out = voxels // tile
    spans = echo.shape[0] // tile
    depth = voxels // lat
    width = depth // chans
    mix_out[0], mix_out[1] = correlation(psf, chans, lat, width, vox_total)
    live = count[0]
    dense[...] = jnp.zeros_like(dense)
    lanes = lax.broadcasted_iota(jnp.int32, (tile, tile), 1)

    def one_batch(turn, carry):
        for lane in range(BATCH):
            at = turn * BATCH + lane
            slot = jnp.minimum(at, slots - 1)
            goal = jnp.where(at < live, target[slot], tiles_out)
            first = offset[slot]
            span, shift = first // tile, first % tile
            turned = pltpu.roll(weights[slot].astype(F32), shift, 1)
            dense[goal, span] += jnp.where(lanes >= shift, turned, 0.0)
            dense[goal, span + 1] += jnp.where(lanes < shift, turned, 0.0)
        return carry

    turns = (live + BATCH - 1) // BATCH
    for i in range(CHUNKS):
        copies[i].wait()
        last = jnp.minimum(turns, (i + 1) * chunk // BATCH)
        lax.fori_loop(i * chunk // BATCH, last, one_batch, 0)
    copies[CHUNKS].wait()

    rows = []
    for t in range(tiles_out):
        rows.append(jnp.concatenate([dense[t, s] for s in range(spans)], axis=1))
    high, low = split(jnp.concatenate(rows, axis=0))
    data = echo[...].reshape(echo.shape[0], 2 * echo.shape[2])
    sums = dot(high, data) + dot(low, data)
    voxel_ids = lax.broadcasted_iota(jnp.int32, (voxels, voxels), 0)
    placing = (voxel_ids == grid_map[...]).astype(F32).astype(BF16)
    high, low = split(sums)
    arranged[...] = dot(placing, high, ((0,), (0,))) + dot(placing, low, ((0,), (0,)))
    mine = lax.axis_index("chan")
    for a in range(lat):
        for step in range(chans):
            first = pl.multiple_of(a * depth + (mine ^ step) * width, 8)
            rows = arranged[pl.ds(first, width), :]
            if step == 0:
                own_out[a * width : (a + 1) * width, :] = rows
            else:
                send_out[step - 1, a * width : (a + 1) * width, :] = rows.astype(BF16)


def gram_parts(a, b):
    con = ((0,), (0,))
    return [dot(a, a, con), dot(a, b, con), dot(b, b, con)]


def gram_kernel(*refs):
    out = refs[-1]
    count = (len(refs) - 1) // 2
    a = jnp.concatenate([r[...] for r in refs[:count]], axis=0)
    b = jnp.concatenate([r[...] for r in refs[count : 2 * count]], axis=0)
    for i, t in enumerate(gram_parts(a, b)):
        out[i] = t


def neighbours(chan, chans, width):
    if chans == 1:
        return []
    if chans == 2:
        start = jnp.where(chan == 0, 0, width - EDGE)
        return [(1, start, jnp.where(chan == 0, width, 0) + start)]
    sides = []
    for side in (-1, 1):
        near = jnp.clip(chan + side, 0, chans - 1)
        start = 0 if side == 1 else width - EDGE
        sides.append((chan ^ near, start, jnp.where(near == chan, OUTSIDE, near * width + start)))
    return sides


def correlation(psf, chans, lat, width, vox_total):
    vox = lax.axis_index("vox")
    chan = lax.axis_index("chan")
    n = lat * width
    lat_all = lat + 2 * HALO
    rows = lat_all * width
    sides = neighbours(chan, chans, width)
    total = rows + len(sides) * lat_all * EDGE
    outs = lax.broadcasted_iota(jnp.int32, (n, total), 0)
    ins = lax.broadcasted_iota(jnp.int32, (n, total), 1)
    lat_in = ins // width
    dep_in = chan * width + ins % width
    for s, (_, _, base) in enumerate(sides):
        local = ins - rows - s * lat_all * EDGE
        here = local >= 0
        lat_in = jnp.where(here, local // EDGE, lat_in)
        dep_in = jnp.where(here, base + local % EDGE, dep_in)
    tap_a = lat_in - outs // width
    tap_b = dep_in - (chan * width + outs % width) + HALO
    lat_grid = vox * lat + lat_in - HALO
    inside = (lat_grid >= 0) & (lat_grid < vox_total * lat)
    taps = 2 * HALO + 1
    valid = inside & (tap_a >= 0) & (tap_a < taps) & (tap_b >= 0) & (tap_b < taps)
    tap = jnp.where(valid, tap_a * taps + tap_b, -1)
    mix = jnp.zeros((n, total), F32)
    for i in range(taps):
        for j in range(taps):
            mix = jnp.where(tap == i * taps + j, psf[i, j], mix)
    return split(mix)


def filter_kernel(mix, *refs, fresh, inner, chans, lat, width, vox_total, frames):
    total_blocks = (len(refs) - 3) // 2
    gram = refs[2 * total_blocks] if not fresh else None
    mine = refs[:total_blocks]
    other = refs[total_blocks : 2 * total_blocks]
    out, mat_high, mat_low = refs[-3:]
    n = lat * width
    half = mine[0].shape[1]
    hf = half // 2
    vox = lax.axis_index("vox")
    chan = lax.axis_index("chan")
    if fresh:
        a = jnp.concatenate([r[...] for r in mine[:fresh]], axis=0)
        b = jnp.concatenate([r[...] for r in other[:fresh]], axis=0)
        parts = gram_parts(a, b)
    else:
        parts = [gram[i] for i in range(3)]

    def diag_sum(t):
        r = lax.broadcasted_iota(jnp.int32, (DIAG, DIAG), 0)
        c = lax.broadcasted_iota(jnp.int32, (DIAG, DIAG), 1)
        tiles = [t[i : i + DIAG, i : i + DIAG] for i in range(0, half, DIAG)]
        return jnp.sum(jnp.where(r == c, functools.reduce(jnp.add, tiles), 0.0))

    factor = frames / (diag_sum(parts[0]) + diag_sum(parts[2]))
    for i, t in enumerate(parts):
        real = t[:hf, :hf] + t[hf:, hf:]
        imag = t[:hf, hf:] - t[hf:, :hf]
        real_high, real_low = split(real)
        imag_high, imag_low = split(imag)
        for ref, re, im in ((mat_high, real_high, imag_high), (mat_low, real_low, imag_low)):
            ref[i, :hf, :hf] = re
            ref[i, hf:, hf:] = re
            ref[i, :hf, hf:] = im
            ref[i, hf:, :hf] = -im

    edge = HALO * width

    def border(blocks, v, away, cut):
        if vox_total > inner:
            return blocks[(inner if v < 0 else inner + 1) * chans + away][cut, :]
        distance = vox ^ jnp.clip(vox + v, 0, vox_total - 1)
        rows = blocks[away][cut, :].astype(F32)
        for d in range(1, inner):
            rows = jnp.where(distance == d, blocks[d * chans + away][cut, :].astype(F32), rows)
        return rows.astype(BF16)

    def column(blocks, away):
        return jnp.concatenate(
            [
                border(blocks, -1, away, slice(n - edge, n)),
                blocks[away][...],
                border(blocks, 1, away, slice(0, edge)),
            ],
            axis=0,
        )

    def any_column(blocks, away):
        if isinstance(away, int):
            return column(blocks, away)
        got = column(blocks, 0).astype(F32)
        for d in range(1, chans):
            got = jnp.where(away == d, column(blocks, d).astype(F32), got)
        return got.astype(BF16)

    lat_all = lat + 2 * HALO
    rows = lat_all * width
    pr = lax.broadcasted_iota(jnp.int32, (lat_all * EDGE, rows), 0)
    pc = lax.broadcasted_iota(jnp.int32, (lat_all * EDGE, rows), 1)
    x_rows = [[column(mine, 0)], [column(other, 0)]]
    for away, start, _ in neighbours(chan, chans, width):
        pick = (pr // EDGE == pc // width) & (pc % width == start + pr % EDGE)
        pick = pick.astype(F32).astype(BF16)
        for which, blocks in enumerate((mine, other)):
            x_rows[which].append(dot(pick, any_column(blocks, away)).astype(BF16))
    xa, xb = (jnp.concatenate(x, axis=0) for x in x_rows)

    def product(z, i, back=False):
        high, low = mat_high[i], mat_low[i]
        if len(z) == 1:
            left, right = [z[0]], [high]
        else:
            left, right = [z[0], z[1], z[0]], [high, high, low]
        axis = 1 if back else 0
        return dot(
            jnp.concatenate(left, axis=1), jnp.concatenate(right, axis=axis), ((1,), (axis,))
        )

    c0, c1, c2, c3 = POLY_COEFFS
    fa, fb = xa.astype(F32), xb.astype(F32)
    first = c3 * factor
    za = first * (product([xa], 0) + product([xb], 1, True)) + c2 * fa
    zb = first * (product([xa], 1) + product([xb], 2)) + c2 * fb
    sa, sb = split(za), split(zb)
    za = factor * (product(sa, 0) + product(sb, 1, True)) + c1 * fa
    zb = factor * (product(sa, 1) + product(sb, 2)) + c1 * fb
    sa, sb = split(za), split(zb)
    za = factor * (product(sa, 0) + product(sb, 1, True)) + c0 * fa
    env = jnp.sqrt(za[:, :hf] * za[:, :hf] + za[:, hf:] * za[:, hf:] + 1e-06)
    eh, el = split(env)
    mh, ml = mix[0], mix[1]
    out[...] = dot(mh, eh) + dot(ml, eh) + dot(mh, el)


def shards(mesh, echo_data, tile_weights, tile_target, tile_offset, tile_count, grid_map, psf_kernel):
    rows, hf = echo_data.shape[2], echo_data.shape[4]
    slots, tile = tile_weights.shape[2], tile_weights.shape[3]
    voxels = grid_map.shape[1]
    chans, vox_total, frms = mesh.shape["chan"], mesh.shape["vox"], mesh.shape["frm"]
    lat = 8
    width = voxels // lat // chans
    n = lat * width
    smem = pl.BlockSpec(memory_space=pltpu.SMEM)
    vmem = pl.BlockSpec(memory_space=pltpu.VMEM)
    hbm = pl.BlockSpec(memory_space=pl.ANY)
    echo = echo_data.reshape(rows, 2, hf)
    seen = (lat + 2 * HALO) * (width + min(chans - 1, 2) * EDGE)
    own, sent, mix = pl.pallas_call(
        functools.partial(das_kernel, chans=chans, lat=lat, vox_total=vox_total),
        out_shape=(
            pltpu.VMEM((n, 2 * hf), F32),
            pltpu.VMEM((chans - 1, n, 2 * hf), BF16),
            pltpu.VMEM((2, n, seen), BF16),
        ),
        in_specs=[smem, smem, smem, hbm, hbm, vmem, smem],
        out_specs=(vmem, vmem, vmem),
        scratch_shapes=[
            pltpu.VMEM((rows, 2, hf), BF16),
            pltpu.VMEM((slots, tile, tile), BF16),
            pltpu.VMEM((voxels // tile + 1, rows // tile + 1, tile, tile), F32),
            pltpu.VMEM((voxels, 2 * hf), F32),
            pltpu.SemaphoreType.DMA((CHUNKS + 1,)),
        ],
        compiler_params=pltpu.CompilerParams(vmem_limit_bytes=56 * 2**20),
    )(
        tile_count.reshape(-1),
        tile_target.reshape(-1),
        tile_offset.reshape(-1),
        echo,
        tile_weights.reshape(slots, tile, tile),
        grid_map,
        psf_kernel,
    )
    inner = min(vox_total, 4)

    def peer(x, dv, dc):
        pairs = [
            (v * chans + c, (v ^ dv) * chans + (c ^ dc))
            for v in range(vox_total)
            for c in range(chans)
        ]
        return lax.ppermute(x, ("vox", "chan"), pairs)

    for step in range(1, chans):
        own = own + peer(sent[step - 1], 0, step).astype(F32)
    own = own.astype(BF16)
    crossed = peer(own, inner // 2, 0)
    near = [(dv, dc) for dv in range(inner // 2) for dc in range(chans)]
    mine = [own] + [peer(own, dv, dc) for dv, dc in near[1:]]
    mine += [crossed] + [peer(crossed, dv, dc) for dv, dc in near[1:]]

    def to_other(x):
        return lax.ppermute(x, "frm", [(f, f ^ 1) for f in range(frms)])

    groups = inner * chans
    other = [to_other(x) for x in mine]

    def gram_of(a, b):
        cost = pl.CostEstimate(
            flops=6 * len(a) * n * (2 * hf) ** 2, bytes_accessed=12 * (2 * hf) ** 2, transcendentals=0
        )
        return pl.pallas_call(
            gram_kernel,
            out_shape=jax.ShapeDtypeStruct((3, 2 * hf, 2 * hf), F32),
            in_specs=[vmem] * (2 * len(a)),
            out_specs=vmem,
            cost_estimate=cost,
            compiler_params=pltpu.CompilerParams(vmem_limit_bytes=VMEM_LIMIT),
        )(*a, *b)

    fresh, gram = groups, []
    if vox_total > inner:
        fresh, gram = 0, [gram_of(mine, other)]
        away = inner
        while away < vox_total:
            gram = [gram[0] + peer(gram[0], away, 0)]
            away *= 2
        for go in (1, -1):
            pairs = [(v, v + go) for v in range(vox_total) if 0 <= v + go < vox_total]
            mine += [lax.ppermute(x, "vox", pairs) for x in mine[:chans]]
            other += [lax.ppermute(x, "vox", pairs) for x in other[:chans]]
    blocks = len(mine)
    out = pl.pallas_call(
        functools.partial(
            filter_kernel,
            fresh=fresh,
            inner=inner,
            chans=chans,
            lat=lat,
            width=width,
            vox_total=vox_total,
            frames=float(frms * hf),
        ),
        out_shape=jax.ShapeDtypeStruct((n, hf), F32),
        in_specs=[vmem] * (1 + 2 * blocks + len(gram)),
        out_specs=vmem,
        scratch_shapes=[
            pltpu.VMEM((3, 2 * hf, 2 * hf), BF16),
            pltpu.VMEM((3, 2 * hf, 2 * hf), BF16),
        ],
        compiler_params=pltpu.CompilerParams(vmem_limit_bytes=VMEM_LIMIT),
    )(mix, *mine, *other, *gram)
    return out.reshape(lat, width, hf)


def solution(mesh):
    in_specs = (
        P(("groups", "vox"), "chan", None, None, "frm"),
        P("vox", "chan", None, None, None),
        P("vox", "chan", None),
        P("vox", "chan", None),
        P("vox", "chan"),
        P("vox", None),
        P(),
    )
    out_specs = P(("groups", "vox"), "chan", "frm")
    return jax.shard_map(
        functools.partial(shards, mesh),
        mesh=mesh,
        in_specs=in_specs,
        out_specs=out_specs,
        check_vma=False,
    )
```

```python
import functools

import jax
import jax.numpy as jnp
from jax import lax
from jax.experimental import pallas as pl
from jax.experimental.pallas import tpu as pltpu
from jax.sharding import PartitionSpec as P

POLY_COEFFS = (1.0, -0.6, 0.15, -0.03)
HALO = 2
BATCH = 8
CHUNKS = 4
EDGE = 2
DIAG = 128
OUTSIDE = -(10**6)
VMEM_LIMIT = 24 * 2**20
F32 = jnp.float32
BF16 = jnp.bfloat16


def split(x):
    high = x.astype(BF16)
    return high, (x - high.astype(F32)).astype(BF16)


def dot(a, b, dims=((1,), (0,))):
    return lax.dot_general(a, b, (dims, ((), ())), preferred_element_type=F32)


def das_kernel(
    count,
    target,
    offset,
    echo_hbm,
    weights_hbm,
    grid_map,
    psf,
    own_out,
    send_out,
    mix_out,
    echo,
    weights,
    dense,
    arranged,
    sems,
    *,
    chans,
    lat,
    vox_total,
):
    slots, tile = weights.shape[0], weights.shape[1]
    chunk = slots // CHUNKS
    copies = [
        pltpu.make_async_copy(
            weights_hbm.at[pl.ds(i * chunk, chunk)], weights.at[pl.ds(i * chunk, chunk)], sems.at[i]
        )
        for i in range(CHUNKS)
    ]
    copies.append(pltpu.make_async_copy(echo_hbm, echo, sems.at[CHUNKS]))
    for copy in copies:
        copy.start()
    voxels = grid_map.shape[1]
    tiles_out = voxels // tile
    spans = echo.shape[0] // tile
    depth = voxels // lat
    width = depth // chans
    mix_out[0], mix_out[1] = correlation(psf, chans, lat, width, vox_total)
    live = count[0]
    dense[...] = jnp.zeros_like(dense)
    lanes = lax.broadcasted_iota(jnp.int32, (tile, tile), 1)

    def one_batch(turn, carry):
        for lane in range(BATCH):
            at = turn * BATCH + lane
            slot = jnp.minimum(at, slots - 1)
            goal = jnp.where(at < live, target[slot], tiles_out)
            first = offset[slot]
            span, shift = first // tile, first % tile
            turned = pltpu.roll(weights[slot].astype(F32), shift, 1)
            dense[goal, span] += jnp.where(lanes >= shift, turned, 0.0)
            dense[goal, span + 1] += jnp.where(lanes < shift, turned, 0.0)
        return carry

    turns = (live + BATCH - 1) // BATCH
    for i in range(CHUNKS):
        copies[i].wait()
        last = jnp.minimum(turns, (i + 1) * chunk // BATCH)
        lax.fori_loop(i * chunk // BATCH, last, one_batch, 0)
    copies[CHUNKS].wait()

    rows = []
    for t in range(tiles_out):
        rows.append(jnp.concatenate([dense[t, s] for s in range(spans)], axis=1))
    high, low = split(jnp.concatenate(rows, axis=0))
    data = echo[...].reshape(echo.shape[0], 2 * echo.shape[2])
    sums = dot(high, data) + dot(low, data)
    voxel_ids = lax.broadcasted_iota(jnp.int32, (voxels, voxels), 0)
    placing = (voxel_ids == grid_map[...]).astype(F32).astype(BF16)
    high, low = split(sums)
    arranged[...] = dot(placing, high, ((0,), (0,))) + dot(placing, low, ((0,), (0,)))
    mine = lax.axis_index("chan")
    for a in range(lat):
        for step in range(chans):
            first = pl.multiple_of(a * depth + (mine ^ step) * width, 8)
            rows = arranged[pl.ds(first, width), :]
            if step == 0:
                own_out[a * width : (a + 1) * width, :] = rows
            else:
                send_out[step - 1, a * width : (a + 1) * width, :] = rows.astype(BF16)


def gram_parts(a, b):
    con = ((0,), (0,))
    return [dot(a, a, con), dot(a, b, con), dot(b, b, con)]


def gram_kernel(*refs):
    out = refs[-1]
    count = (len(refs) - 1) // 2
    a = jnp.concatenate([r[...] for r in refs[:count]], axis=0)
    b = jnp.concatenate([r[...] for r in refs[count : 2 * count]], axis=0)
    for i, t in enumerate(gram_parts(a, b)):
        out[i] = t


def neighbours(chan, chans, width):
    if chans == 1:
        return []
    if chans == 2:
        start = jnp.where(chan == 0, 0, width - EDGE)
        return [(1, start, jnp.where(chan == 0, width, 0) + start)]
    sides = []
    for side in (-1, 1):
        near = jnp.clip(chan + side, 0, chans - 1)
        start = 0 if side == 1 else width - EDGE
        sides.append((chan ^ near, start, jnp.where(near == chan, OUTSIDE, near * width + start)))
    return sides


def correlation(psf, chans, lat, width, vox_total):
    vox = lax.axis_index("vox")
    chan = lax.axis_index("chan")
    n = lat * width
    lat_all = lat + 2 * HALO
    rows = lat_all * width
    sides = neighbours(chan, chans, width)
    total = rows + len(sides) * lat_all * EDGE
    outs = lax.broadcasted_iota(jnp.int32, (n, total), 0)
    ins = lax.broadcasted_iota(jnp.int32, (n, total), 1)
    lat_in = ins // width
    dep_in = chan * width + ins % width
    for s, (_, _, base) in enumerate(sides):
        local = ins - rows - s * lat_all * EDGE
        here = local >= 0
        lat_in = jnp.where(here, local // EDGE, lat_in)
        dep_in = jnp.where(here, base + local % EDGE, dep_in)
    tap_a = lat_in - outs // width
    tap_b = dep_in - (chan * width + outs % width) + HALO
    lat_grid = vox * lat + lat_in - HALO
    inside = (lat_grid >= 0) & (lat_grid < vox_total * lat)
    taps = 2 * HALO + 1
    valid = inside & (tap_a >= 0) & (tap_a < taps) & (tap_b >= 0) & (tap_b < taps)
    tap = jnp.where(valid, tap_a * taps + tap_b, -1)
    mix = jnp.zeros((n, total), F32)
    for i in range(taps):
        for j in range(taps):
            mix = jnp.where(tap == i * taps + j, psf[i, j], mix)
    return split(mix)


def filter_kernel(mix, *refs, fresh, inner, chans, lat, width, vox_total, frames):
    total_blocks = (len(refs) - 3) // 2
    gram = refs[2 * total_blocks] if not fresh else None
    mine = refs[:total_blocks]
    other = refs[total_blocks : 2 * total_blocks]
    out, mat_high, mat_low = refs[-3:]
    n = lat * width
    half = mine[0].shape[1]
    hf = half // 2
    vox = lax.axis_index("vox")
    chan = lax.axis_index("chan")
    if fresh:
        a = jnp.concatenate([r[...] for r in mine[:fresh]], axis=0)
        b = jnp.concatenate([r[...] for r in other[:fresh]], axis=0)
        parts = gram_parts(a, b)
    else:
        parts = [gram[i] for i in range(3)]

    def diag_sum(t):
        r = lax.broadcasted_iota(jnp.int32, (DIAG, DIAG), 0)
        c = lax.broadcasted_iota(jnp.int32, (DIAG, DIAG), 1)
        tiles = [t[i : i + DIAG, i : i + DIAG] for i in range(0, half, DIAG)]
        return jnp.sum(jnp.where(r == c, functools.reduce(jnp.add, tiles), 0.0))

    factor = frames / (diag_sum(parts[0]) + diag_sum(parts[2]))
    for i, t in enumerate(parts):
        real = t[:hf, :hf] + t[hf:, hf:]
        imag = t[:hf, hf:] - t[hf:, :hf]
        real_high, real_low = split(real)
        imag_high, imag_low = split(imag)
        for ref, re, im in ((mat_high, real_high, imag_high), (mat_low, real_low, imag_low)):
            ref[i, :hf, :hf] = re
            ref[i, hf:, hf:] = re
            ref[i, :hf, hf:] = im
            ref[i, hf:, :hf] = -im

    edge = HALO * width

    def border(blocks, v, away, cut):
        if vox_total > inner:
            return blocks[(inner if v < 0 else inner + 1) * chans + away][cut, :]
        distance = vox ^ jnp.clip(vox + v, 0, vox_total - 1)
        rows = blocks[away][cut, :].astype(F32)
        for d in range(1, inner):
            rows = jnp.where(distance == d, blocks[d * chans + away][cut, :].astype(F32), rows)
        return rows.astype(BF16)

    def column(blocks, away):
        return jnp.concatenate(
            [
                border(blocks, -1, away, slice(n - edge, n)),
                blocks[away][...],
                border(blocks, 1, away, slice(0, edge)),
            ],
            axis=0,
        )

    def any_column(blocks, away):
        if isinstance(away, int):
            return column(blocks, away)
        got = column(blocks, 0).astype(F32)
        for d in range(1, chans):
            got = jnp.where(away == d, column(blocks, d).astype(F32), got)
        return got.astype(BF16)

    lat_all = lat + 2 * HALO
    rows = lat_all * width
    pr = lax.broadcasted_iota(jnp.int32, (lat_all * EDGE, rows), 0)
    pc = lax.broadcasted_iota(jnp.int32, (lat_all * EDGE, rows), 1)
    x_rows = [[column(mine, 0)], [column(other, 0)]]
    for away, start, _ in neighbours(chan, chans, width):
        pick = (pr // EDGE == pc // width) & (pc % width == start + pr % EDGE)
        pick = pick.astype(F32).astype(BF16)
        for which, blocks in enumerate((mine, other)):
            x_rows[which].append(dot(pick, any_column(blocks, away)).astype(BF16))
    xa, xb = (jnp.concatenate(x, axis=0) for x in x_rows)

    def product(z, i, back=False):
        high, low = mat_high[i], mat_low[i]
        if len(z) == 1:
            left, right = [z[0]], [high]
        else:
            left, right = [z[0], z[1], z[0]], [high, high, low]
        axis = 1 if back else 0
        return dot(
            jnp.concatenate(left, axis=1), jnp.concatenate(right, axis=axis), ((1,), (axis,))
        )

    c0, c1, c2, c3 = POLY_COEFFS
    fa, fb = xa.astype(F32), xb.astype(F32)
    first = c3 * factor
    za = first * (product([xa], 0) + product([xb], 1, True)) + c2 * fa
    zb = first * (product([xa], 1) + product([xb], 2)) + c2 * fb
    sa, sb = split(za), split(zb)
    za = factor * (product(sa, 0) + product(sb, 1, True)) + c1 * fa
    zb = factor * (product(sa, 1) + product(sb, 2)) + c1 * fb
    sa, sb = split(za), split(zb)
    za = factor * (product(sa, 0) + product(sb, 1, True)) + c0 * fa
    env = jnp.sqrt(za[:, :hf] * za[:, :hf] + za[:, hf:] * za[:, hf:] + 1e-06)
    eh, el = split(env)
    mh, ml = mix[0], mix[1]
    out[...] = dot(mh, eh) + dot(ml, eh) + dot(mh, el)


def shards(mesh, echo_data, tile_weights, tile_target, tile_offset, tile_count, grid_map, psf_kernel):
    rows, hf = echo_data.shape[2], echo_data.shape[4]
    slots, tile = tile_weights.shape[2], tile_weights.shape[3]
    voxels = grid_map.shape[1]
    chans, vox_total, frms = mesh.shape["chan"], mesh.shape["vox"], mesh.shape["frm"]
    lat = 8
    width = voxels // lat // chans
    n = lat * width
    smem = pl.BlockSpec(memory_space=pltpu.SMEM)
    vmem = pl.BlockSpec(memory_space=pltpu.VMEM)
    hbm = pl.BlockSpec(memory_space=pl.ANY)
    echo = echo_data.reshape(rows, 2, hf)
    seen = (lat + 2 * HALO) * (width + min(chans - 1, 2) * EDGE)
    own, sent, mix = pl.pallas_call(
        functools.partial(das_kernel, chans=chans, lat=lat, vox_total=vox_total),
        out_shape=(
            pltpu.VMEM((n, 2 * hf), F32),
            pltpu.VMEM((chans - 1, n, 2 * hf), BF16),
            pltpu.VMEM((2, n, seen), BF16),
        ),
        in_specs=[smem, smem, smem, hbm, hbm, vmem, smem],
        out_specs=(vmem, vmem, vmem),
        scratch_shapes=[
            pltpu.VMEM((rows, 2, hf), BF16),
            pltpu.VMEM((slots, tile, tile), BF16),
            pltpu.VMEM((voxels // tile + 1, rows // tile + 1, tile, tile), F32),
            pltpu.VMEM((voxels, 2 * hf), F32),
            pltpu.SemaphoreType.DMA((CHUNKS + 1,)),
        ],
        compiler_params=pltpu.CompilerParams(vmem_limit_bytes=56 * 2**20),
    )(
        tile_count.reshape(-1),
        tile_target.reshape(-1),
        tile_offset.reshape(-1),
        echo,
        tile_weights.reshape(slots, tile, tile),
        grid_map,
        psf_kernel,
    )
    inner = min(vox_total, 4)

    def peer(x, dv, dc):
        pairs = [
            (v * chans + c, (v ^ dv) * chans + (c ^ dc))
            for v in range(vox_total)
            for c in range(chans)
        ]
        return lax.ppermute(x, ("vox", "chan"), pairs)

    for step in range(1, chans):
        own = own + peer(sent[step - 1], 0, step).astype(F32)
    own = own.astype(BF16)
    crossed = peer(own, inner // 2, 0)
    near = [(dv, dc) for dv in range(inner // 2) for dc in range(chans)]
    mine = [own] + [peer(own, dv, dc) for dv, dc in near[1:]]
    mine += [crossed] + [peer(crossed, dv, dc) for dv, dc in near[1:]]

    def to_other(x):
        return lax.ppermute(x, "frm", [(f, f ^ 1) for f in range(frms)])

    groups = inner * chans
    part = groups // 2
    tied = lax.optimization_barrier(tuple(mine[1:part] + mine[part + 1 : part + 3]))
    mine = [mine[0], *tied[: part - 1], mine[part], *tied[part - 1 :], *mine[part + 3 :]]
    other = [to_other(x) for x in mine]

    def gram_of(a, b):
        cost = pl.CostEstimate(
            flops=6 * len(a) * n * (2 * hf) ** 2, bytes_accessed=12 * (2 * hf) ** 2, transcendentals=0
        )
        return pl.pallas_call(
            gram_kernel,
            out_shape=jax.ShapeDtypeStruct((3, 2 * hf, 2 * hf), F32),
            in_specs=[vmem] * (2 * len(a)),
            out_specs=vmem,
            cost_estimate=cost,
            compiler_params=pltpu.CompilerParams(vmem_limit_bytes=VMEM_LIMIT),
        )(*a, *b)

    fresh, gram = groups, []
    if vox_total > inner:
        fresh, gram = 0, [gram_of(mine, other)]
        away = inner
        while away < vox_total:
            gram = [gram[0] + peer(gram[0], away, 0)]
            away *= 2
        for go in (1, -1):
            pairs = [(v, v + go) for v in range(vox_total) if 0 <= v + go < vox_total]
            mine += [lax.ppermute(x, "vox", pairs) for x in mine[:chans]]
            other += [lax.ppermute(x, "vox", pairs) for x in other[:chans]]
    blocks = len(mine)
    out = pl.pallas_call(
        functools.partial(
            filter_kernel,
            fresh=fresh,
            inner=inner,
            chans=chans,
            lat=lat,
            width=width,
            vox_total=vox_total,
            frames=float(frms * hf),
        ),
        out_shape=jax.ShapeDtypeStruct((n, hf), F32),
        in_specs=[vmem] * (1 + 2 * blocks + len(gram)),
        out_specs=vmem,
        scratch_shapes=[
            pltpu.VMEM((3, 2 * hf, 2 * hf), BF16),
            pltpu.VMEM((3, 2 * hf, 2 * hf), BF16),
        ],
        compiler_params=pltpu.CompilerParams(vmem_limit_bytes=VMEM_LIMIT),
    )(mix, *mine, *other, *gram)
    return out.reshape(lat, width, hf)


def solution(mesh):
    in_specs = (
        P(("groups", "vox"), "chan", None, None, "frm"),
        P("vox", "chan", None, None, None),
        P("vox", "chan", None),
        P("vox", "chan", None),
        P("vox", "chan"),
        P("vox", None),
        P(),
    )
    out_specs = P(("groups", "vox"), "chan", "frm")
    return jax.shard_map(
        functools.partial(shards, mesh),
        mesh=mesh,
        in_specs=in_specs,
        out_specs=out_specs,
        check_vma=False,
    )
```

```python
import functools

import jax
import jax.numpy as jnp
from jax import lax
from jax.experimental import pallas as pl
from jax.experimental.pallas import tpu as pltpu
from jax.sharding import PartitionSpec as P

POLY_COEFFS = (1.0, -0.6, 0.15, -0.03)
HALO = 2
BATCH = 8
CHUNKS = 4
EDGE = 2
DIAG = 128
OUTSIDE = -(10**6)
VMEM_LIMIT = 24 * 2**20
F32 = jnp.float32
BF16 = jnp.bfloat16


def split(x):
    high = x.astype(BF16)
    return high, (x - high.astype(F32)).astype(BF16)


def dot(a, b, dims=((1,), (0,))):
    return lax.dot_general(a, b, (dims, ((), ())), preferred_element_type=F32)


def das_kernel(
    count,
    target,
    offset,
    echo_hbm,
    weights_hbm,
    grid_map,
    psf,
    own_out,
    send_out,
    mix_out,
    echo,
    weights,
    dense,
    arranged,
    sems,
    *,
    chans,
    lat,
    vox_total,
):
    slots, tile = weights.shape[0], weights.shape[1]
    chunk = slots // CHUNKS
    copies = [
        pltpu.make_async_copy(
            weights_hbm.at[pl.ds(i * chunk, chunk)], weights.at[pl.ds(i * chunk, chunk)], sems.at[i]
        )
        for i in range(CHUNKS)
    ]
    copies.append(pltpu.make_async_copy(echo_hbm, echo, sems.at[CHUNKS]))
    for copy in copies:
        copy.start()
    voxels = grid_map.shape[1]
    tiles_out = voxels // tile
    spans = echo.shape[0] // tile
    depth = voxels // lat
    width = depth // chans
    mix_out[0], mix_out[1] = correlation(psf, chans, lat, width, vox_total)
    live = count[0, 0]
    dense[...] = jnp.zeros_like(dense)
    lanes = lax.broadcasted_iota(jnp.int32, (tile, tile), 1)

    def one_batch(turn, carry):
        for lane in range(BATCH):
            at = turn * BATCH + lane
            slot = jnp.minimum(at, slots - 1)
            goal = jnp.where(at < live, target[slot], tiles_out)
            first = offset[slot]
            span, shift = first // tile, first % tile
            turned = pltpu.roll(weights[slot].astype(F32), shift, 1)
            dense[goal, span] += jnp.where(lanes >= shift, turned, 0.0)
            dense[goal, span + 1] += jnp.where(lanes < shift, turned, 0.0)
        return carry

    turns = (live + BATCH - 1) // BATCH
    for i in range(CHUNKS):
        copies[i].wait()
        last = jnp.minimum(turns, (i + 1) * chunk // BATCH)
        lax.fori_loop(i * chunk // BATCH, last, one_batch, 0)
    copies[CHUNKS].wait()

    rows = []
    for t in range(tiles_out):
        rows.append(jnp.concatenate([dense[t, s] for s in range(spans)], axis=1))
    high, low = split(jnp.concatenate(rows, axis=0))
    data = echo[...].reshape(echo.shape[0], 2 * echo.shape[2])
    sums = dot(high, data) + dot(low, data)
    voxel_ids = lax.broadcasted_iota(jnp.int32, (voxels, voxels), 0)
    placing = (voxel_ids == grid_map[...]).astype(F32).astype(BF16)
    high, low = split(sums)
    arranged[...] = dot(placing, high, ((0,), (0,))) + dot(placing, low, ((0,), (0,)))
    mine = lax.axis_index("chan")
    for a in range(lat):
        for step in range(chans):
            first = pl.multiple_of(a * depth + (mine ^ step) * width, 8)
            rows = arranged[pl.ds(first, width), :]
            if step == 0:
                own_out[a * width : (a + 1) * width, :] = rows
            else:
                send_out[step - 1, a * width : (a + 1) * width, :] = rows


def gram_parts(a, b):
    hf = a.shape[1] // 2
    con = ((0,), (0,))
    a_real, a_imag, b_real, b_imag = a[:, :hf], a[:, hf:], b[:, :hf], b[:, hf:]
    a_all = jnp.concatenate([a_real, a_imag], axis=0)
    b_all = jnp.concatenate([b_real, b_imag], axis=0)
    aa, bb = dot(a_real, a_imag, con), dot(b_real, b_imag, con)
    return [
        (dot(a_all, a_all, con), aa - aa.T),
        (dot(a_all, b_all, con), dot(a_real, b_imag, con) - dot(a_imag, b_real, con)),
        (dot(b_all, b_all, con), bb - bb.T),
    ]


def gram_kernel(*refs):
    out = refs[-1]
    count = (len(refs) - 1) // 2
    a = jnp.concatenate([r[...] for r in refs[:count]], axis=0)
    b = jnp.concatenate([r[...] for r in refs[count : 2 * count]], axis=0)
    for i, (real, imag) in enumerate(gram_parts(a, b)):
        out[i, 0], out[i, 1] = real, imag


def neighbours(chan, chans, width):
    if chans == 1:
        return []
    if chans == 2:
        start = jnp.where(chan == 0, 0, width - EDGE)
        return [(1, start, jnp.where(chan == 0, width, 0) + start)]
    sides = []
    for side in (-1, 1):
        near = jnp.clip(chan + side, 0, chans - 1)
        start = 0 if side == 1 else width - EDGE
        sides.append((chan ^ near, start, jnp.where(near == chan, OUTSIDE, near * width + start)))
    return sides


def correlation(psf, chans, lat, width, vox_total):
    vox = lax.axis_index("vox")
    chan = lax.axis_index("chan")
    n = lat * width
    lat_all = lat + 2 * HALO
    rows = lat_all * width
    sides = neighbours(chan, chans, width)
    total = rows + len(sides) * lat_all * EDGE
    outs = lax.broadcasted_iota(jnp.int32, (n, total), 0)
    ins = lax.broadcasted_iota(jnp.int32, (n, total), 1)
    lat_in = ins // width
    dep_in = chan * width + ins % width
    for s, (_, _, base) in enumerate(sides):
        local = ins - rows - s * lat_all * EDGE
        here = local >= 0
        lat_in = jnp.where(here, local // EDGE, lat_in)
        dep_in = jnp.where(here, base + local % EDGE, dep_in)
    tap_a = lat_in - outs // width
    tap_b = dep_in - (chan * width + outs % width) + HALO
    lat_grid = vox * lat + lat_in - HALO
    inside = (lat_grid >= 0) & (lat_grid < vox_total * lat)
    taps = 2 * HALO + 1
    valid = inside & (tap_a >= 0) & (tap_a < taps) & (tap_b >= 0) & (tap_b < taps)
    tap = jnp.where(valid, tap_a * taps + tap_b, -1)
    mix = jnp.zeros((n, total), F32)
    for i in range(taps):
        for j in range(taps):
            mix = jnp.where(tap == i * taps + j, psf[i, j], mix)
    return split(mix)


def filter_kernel(mix, *refs, fresh, inner, chans, lat, width, vox_total, frames):
    total_blocks = (len(refs) - 3) // 2
    gram = refs[2 * total_blocks] if not fresh else None
    mine = refs[:total_blocks]
    other = refs[total_blocks : 2 * total_blocks]
    out, mat_high, mat_low = refs[-3:]
    n = lat * width
    half = mine[0].shape[1]
    hf = half // 2
    vox = lax.axis_index("vox")
    chan = lax.axis_index("chan")
    if fresh:
        a = jnp.concatenate([r[...] for r in mine[:fresh]], axis=0)
        b = jnp.concatenate([r[...] for r in other[:fresh]], axis=0)
        parts = gram_parts(a, b)
    else:
        parts = [(gram[i, 0], gram[i, 1]) for i in range(3)]

    def diag_sum(t):
        r = lax.broadcasted_iota(jnp.int32, (DIAG, DIAG), 0)
        c = lax.broadcasted_iota(jnp.int32, (DIAG, DIAG), 1)
        tiles = [t[i : i + DIAG, i : i + DIAG] for i in range(0, hf, DIAG)]
        return jnp.sum(jnp.where(r == c, functools.reduce(jnp.add, tiles), 0.0))

    factor = frames / (diag_sum(parts[0][0]) + diag_sum(parts[2][0]))
    for i, (real, imag) in enumerate(parts):
        real_high, real_low = split(real)
        imag_high, imag_low = split(imag)
        for ref, re, im in ((mat_high, real_high, imag_high), (mat_low, real_low, imag_low)):
            ref[i, :hf, :hf] = re
            ref[i, hf:, hf:] = re
            ref[i, :hf, hf:] = im
            ref[i, hf:, :hf] = -im

    edge = HALO * width

    def border(blocks, v, away, cut):
        if vox_total > inner:
            return blocks[(inner if v < 0 else inner + 1) * chans + away][cut, :]
        distance = vox ^ jnp.clip(vox + v, 0, vox_total - 1)
        rows = blocks[away][cut, :].astype(F32)
        for d in range(1, inner):
            rows = jnp.where(distance == d, blocks[d * chans + away][cut, :].astype(F32), rows)
        return rows.astype(BF16)

    def column(blocks, away):
        return jnp.concatenate(
            [
                border(blocks, -1, away, slice(n - edge, n)),
                blocks[away][...],
                border(blocks, 1, away, slice(0, edge)),
            ],
            axis=0,
        )

    def any_column(blocks, away):
        if isinstance(away, int):
            return column(blocks, away)
        got = column(blocks, 0).astype(F32)
        for d in range(1, chans):
            got = jnp.where(away == d, column(blocks, d).astype(F32), got)
        return got.astype(BF16)

    lat_all = lat + 2 * HALO
    rows = lat_all * width
    pr = lax.broadcasted_iota(jnp.int32, (lat_all * EDGE, rows), 0)
    pc = lax.broadcasted_iota(jnp.int32, (lat_all * EDGE, rows), 1)
    x_rows = [[column(mine, 0)], [column(other, 0)]]
    for away, start, _ in neighbours(chan, chans, width):
        pick = (pr // EDGE == pc // width) & (pc % width == start + pr % EDGE)
        pick = pick.astype(F32).astype(BF16)
        for which, blocks in enumerate((mine, other)):
            x_rows[which].append(dot(pick, any_column(blocks, away)).astype(BF16))
    xa, xb = (jnp.concatenate(x, axis=0) for x in x_rows)

    def product(z, i, back=False):
        high, low = mat_high[i], mat_low[i]
        if len(z) == 1:
            left, right = [z[0]], [high]
        else:
            left, right = [z[0], z[1], z[0]], [high, high, low]
        axis = 1 if back else 0
        return dot(
            jnp.concatenate(left, axis=1), jnp.concatenate(right, axis=axis), ((1,), (axis,))
        )

    c0, c1, c2, c3 = POLY_COEFFS
    fa, fb = xa.astype(F32), xb.astype(F32)
    first = c3 * factor
    za = first * (product([xa], 0) + product([xb], 1, True)) + c2 * fa
    zb = first * (product([xa], 1) + product([xb], 2)) + c2 * fb
    sa, sb = split(za), split(zb)
    za = factor * (product(sa, 0) + product(sb, 1, True)) + c1 * fa
    zb = factor * (product(sa, 1) + product(sb, 2)) + c1 * fb
    sa, sb = split(za), split(zb)
    za = factor * (product(sa, 0) + product(sb, 1, True)) + c0 * fa
    env = jnp.sqrt(za[:, :hf] * za[:, :hf] + za[:, hf:] * za[:, hf:] + 1e-06)
    eh, el = split(env)
    mh, ml = mix[0], mix[1]
    out[...] = dot(mh, eh) + dot(ml, eh) + dot(mh, el)


def shards(mesh, echo_data, tile_weights, tile_target, tile_offset, tile_count, grid_map, psf_kernel):
    rows, hf = echo_data.shape[2], echo_data.shape[4]
    slots, tile = tile_weights.shape[2], tile_weights.shape[3]
    voxels = grid_map.shape[1]
    chans, vox_total, frms = mesh.shape["chan"], mesh.shape["vox"], mesh.shape["frm"]
    lat = 8
    width = voxels // lat // chans
    n = lat * width
    smem = pl.BlockSpec(memory_space=pltpu.SMEM)
    vmem = pl.BlockSpec(memory_space=pltpu.VMEM)
    hbm = pl.BlockSpec(memory_space=pl.ANY)
    echo = echo_data.reshape(rows, 2, hf)
    seen = (lat + 2 * HALO) * (width + min(chans - 1, 2) * EDGE)
    own, sent, mix = pl.pallas_call(
        functools.partial(das_kernel, chans=chans, lat=lat, vox_total=vox_total),
        out_shape=(
            pltpu.VMEM((n, 2 * hf), F32),
            pltpu.VMEM((chans - 1, n, 2 * hf), F32),
            pltpu.VMEM((2, n, seen), BF16),
        ),
        in_specs=[smem, smem, smem, hbm, hbm, vmem, smem],
        out_specs=(vmem, vmem, vmem),
        scratch_shapes=[
            pltpu.VMEM((rows, 2, hf), BF16),
            pltpu.VMEM((slots, tile, tile), BF16),
            pltpu.VMEM((voxels // tile + 1, rows // tile + 1, tile, tile), F32),
            pltpu.VMEM((voxels, 2 * hf), F32),
            pltpu.SemaphoreType.DMA((CHUNKS + 1,)),
        ],
        compiler_params=pltpu.CompilerParams(vmem_limit_bytes=56 * 2**20),
    )(
        tile_count,
        tile_target.reshape(-1),
        tile_offset.reshape(-1),
        echo,
        tile_weights.reshape(slots, tile, tile),
        grid_map,
        psf_kernel,
    )
    inner = min(vox_total, 4)

    def peer(x, dv, dc):
        pairs = [
            (v * chans + c, (v ^ dv) * chans + (c ^ dc))
            for v in range(vox_total)
            for c in range(chans)
        ]
        return lax.ppermute(x, ("vox", "chan"), pairs)

    for step in range(1, chans):
        own = own + peer(sent[step - 1].astype(jnp.float16), 0, step).astype(F32)
    own = own.astype(BF16)
    crossed = peer(own, inner // 2, 0)
    near = [(dv, dc) for dv in range(inner // 2) for dc in range(chans)]
    mine = [own] + [peer(own, dv, dc) for dv, dc in near[1:]]
    mine += [crossed] + [peer(crossed, dv, dc) for dv, dc in near[1:]]

    def to_other(x):
        return lax.ppermute(x, "frm", [(f, f ^ 1) for f in range(frms)])

    groups = inner * chans
    part = groups // 2
    tied = lax.optimization_barrier(tuple(mine[1:part] + mine[part + 1 : part + 3]))
    mine = [mine[0], *tied[: part - 1], mine[part], *tied[part - 1 :], *mine[part + 3 :]]
    other = [to_other(x) for x in mine]

    def gram_of(a, b):
        cost = pl.CostEstimate(
            flops=6 * len(a) * n * (2 * hf) ** 2, bytes_accessed=12 * (2 * hf) ** 2, transcendentals=0
        )
        return pl.pallas_call(
            gram_kernel,
            out_shape=jax.ShapeDtypeStruct((3, 2, hf, hf), F32),
            in_specs=[vmem] * (2 * len(a)),
            out_specs=vmem,
            cost_estimate=cost,
            compiler_params=pltpu.CompilerParams(vmem_limit_bytes=VMEM_LIMIT),
        )(*a, *b)

    fresh, gram = groups, []
    if vox_total > inner:
        fresh, gram = 0, [gram_of(mine, other)]
        away = inner
        while away < vox_total:
            gram = [gram[0] + peer(gram[0], away, 0)]
            away *= 2
        for go in (1, -1):
            pairs = [(v, v + go) for v in range(vox_total) if 0 <= v + go < vox_total]
            mine += [lax.ppermute(x, "vox", pairs) for x in mine[:chans]]
            other += [lax.ppermute(x, "vox", pairs) for x in other[:chans]]
    blocks = len(mine)
    out = pl.pallas_call(
        functools.partial(
            filter_kernel,
            fresh=fresh,
            inner=inner,
            chans=chans,
            lat=lat,
            width=width,
            vox_total=vox_total,
            frames=float(frms * hf),
        ),
        out_shape=jax.ShapeDtypeStruct((n, hf), F32),
        in_specs=[vmem] * (1 + 2 * blocks + len(gram)),
        out_specs=vmem,
        scratch_shapes=[
            pltpu.VMEM((3, 2 * hf, 2 * hf), BF16),
            pltpu.VMEM((3, 2 * hf, 2 * hf), BF16),
        ],
        compiler_params=pltpu.CompilerParams(vmem_limit_bytes=VMEM_LIMIT),
    )(mix, *mine, *other, *gram)
    return out.reshape(lat, width, hf)


def solution(mesh):
    in_specs = (
        P(("groups", "vox"), "chan", None, None, "frm"),
        P("vox", "chan", None, None, None),
        P("vox", "chan", None),
        P("vox", "chan", None),
        P("vox", "chan"),
        P("vox", None),
        P(),
    )
    out_specs = P(("groups", "vox"), "chan", "frm")
    return jax.shard_map(
        functools.partial(shards, mesh),
        mesh=mesh,
        in_specs=in_specs,
        out_specs=out_specs,
        check_vma=False,
    )
```

```python
import functools

import jax
import jax.numpy as jnp
from jax import lax
from jax.experimental import pallas as pl
from jax.experimental.pallas import tpu as pltpu
from jax.sharding import PartitionSpec as P

POLY_COEFFS = (1.0, -0.6, 0.15, -0.03)
HALO = 2
BATCH = 8
CHUNKS = 4
EDGE = 2
DIAG = 128
OUTSIDE = -(10**6)
VMEM_LIMIT = 24 * 2**20
F32 = jnp.float32
BF16 = jnp.bfloat16


def split(x):
    high = x.astype(BF16)
    return high, (x - high.astype(F32)).astype(BF16)


def dot(a, b, dims=((1,), (0,))):
    return lax.dot_general(a, b, (dims, ((), ())), preferred_element_type=F32)


def das_kernel(
    count,
    target,
    offset,
    echo_hbm,
    weights_hbm,
    grid_map,
    psf,
    own_out,
    send_out,
    mix_out,
    echo,
    weights,
    dense,
    arranged,
    sems,
    *,
    chans,
    lat,
    vox_total,
):
    slots, tile = weights.shape[0], weights.shape[1]
    chunk = slots // CHUNKS
    copies = [
        pltpu.make_async_copy(
            weights_hbm.at[pl.ds(i * chunk, chunk)], weights.at[pl.ds(i * chunk, chunk)], sems.at[i]
        )
        for i in range(CHUNKS)
    ]
    copies.append(pltpu.make_async_copy(echo_hbm, echo, sems.at[CHUNKS]))
    for copy in copies:
        copy.start()
    voxels = grid_map.shape[1]
    tiles_out = voxels // tile
    spans = echo.shape[0] // tile
    depth = voxels // lat
    width = depth // chans
    mix_out[0], mix_out[1] = correlation(psf, chans, lat, width, vox_total)
    live = count[0, 0]
    dense[...] = jnp.zeros_like(dense)
    lanes = lax.broadcasted_iota(jnp.int32, (tile, tile), 1)

    def one_batch(turn, carry):
        for lane in range(BATCH):
            at = turn * BATCH + lane
            slot = jnp.minimum(at, slots - 1)
            goal = jnp.where(at < live, target[slot], tiles_out)
            first = offset[slot]
            span, shift = first // tile, first % tile
            turned = pltpu.roll(weights[slot].astype(F32), shift, 1)
            dense[goal, span] += jnp.where(lanes >= shift, turned, 0.0)
            dense[goal, span + 1] += jnp.where(lanes < shift, turned, 0.0)
        return carry

    turns = (live + BATCH - 1) // BATCH
    for i in range(CHUNKS):
        copies[i].wait()
        last = jnp.minimum(turns, (i + 1) * chunk // BATCH)
        lax.fori_loop(i * chunk // BATCH, last, one_batch, 0)
    copies[CHUNKS].wait()

    rows = []
    for t in range(tiles_out):
        rows.append(jnp.concatenate([dense[t, s] for s in range(spans)], axis=1))
    high, low = split(jnp.concatenate(rows, axis=0))
    data = echo[...].reshape(echo.shape[0], 2 * echo.shape[2])
    sums = dot(high, data) + dot(low, data)
    voxel_ids = lax.broadcasted_iota(jnp.int32, (voxels, voxels), 0)
    placing = (voxel_ids == grid_map[...]).astype(F32).astype(BF16)
    high, low = split(sums)
    arranged[...] = dot(placing, high, ((0,), (0,))) + dot(placing, low, ((0,), (0,)))
    mine = lax.axis_index("chan")
    for a in range(lat):
        for step in range(chans):
            first = pl.multiple_of(a * depth + (mine ^ step) * width, 8)
            rows = arranged[pl.ds(first, width), :]
            if step == 0:
                own_out[a * width : (a + 1) * width, :] = rows
            else:
                send_out[step - 1, a * width : (a + 1) * width, :] = rows


def gram_parts(a, b):
    hf = a.shape[1] // 2
    con = ((0,), (0,))
    a_real, a_imag, b_real, b_imag = a[:, :hf], a[:, hf:], b[:, :hf], b[:, hf:]
    a_all = jnp.concatenate([a_real, a_imag], axis=0)
    b_all = jnp.concatenate([b_real, b_imag], axis=0)
    aa, bb = dot(a_real, a_imag, con), dot(b_real, b_imag, con)
    return [
        (dot(a_all, a_all, con), aa - aa.T),
        (dot(a_all, b_all, con), dot(a_real, b_imag, con) - dot(a_imag, b_real, con)),
        (dot(b_all, b_all, con), bb - bb.T),
    ]


def gram_kernel(*refs):
    out = refs[-1]
    count = (len(refs) - 1) // 2
    a = jnp.concatenate([r[...] for r in refs[:count]], axis=0)
    b = jnp.concatenate([r[...] for r in refs[count : 2 * count]], axis=0)
    for i, (real, imag) in enumerate(gram_parts(a, b)):
        out[i, 0], out[i, 1] = real, imag


def neighbours(chan, chans, width):
    if chans == 1:
        return []
    if chans == 2:
        start = jnp.where(chan == 0, 0, width - EDGE)
        return [(1, start, jnp.where(chan == 0, width, 0) + start)]
    sides = []
    for side in (-1, 1):
        near = jnp.clip(chan + side, 0, chans - 1)
        start = 0 if side == 1 else width - EDGE
        sides.append((chan ^ near, start, jnp.where(near == chan, OUTSIDE, near * width + start)))
    return sides


def correlation(psf, chans, lat, width, vox_total):
    vox = lax.axis_index("vox")
    chan = lax.axis_index("chan")
    n = lat * width
    lat_all = lat + 2 * HALO
    rows = lat_all * width
    sides = neighbours(chan, chans, width)
    total = rows + len(sides) * lat_all * EDGE
    outs = lax.broadcasted_iota(jnp.int32, (n, total), 0)
    ins = lax.broadcasted_iota(jnp.int32, (n, total), 1)
    lat_in = ins // width
    dep_in = chan * width + ins % width
    for s, (_, _, base) in enumerate(sides):
        local = ins - rows - s * lat_all * EDGE
        here = local >= 0
        lat_in = jnp.where(here, local // EDGE, lat_in)
        dep_in = jnp.where(here, base + local % EDGE, dep_in)
    tap_a = lat_in - outs // width
    tap_b = dep_in - (chan * width + outs % width) + HALO
    lat_grid = vox * lat + lat_in - HALO
    inside = (lat_grid >= 0) & (lat_grid < vox_total * lat)
    taps = 2 * HALO + 1
    valid = inside & (tap_a >= 0) & (tap_a < taps) & (tap_b >= 0) & (tap_b < taps)
    tap = jnp.where(valid, tap_a * taps + tap_b, -1)
    mix = jnp.zeros((n, total), F32)
    for i in range(taps):
        for j in range(taps):
            mix = jnp.where(tap == i * taps + j, psf[i, j], mix)
    return split(mix)


def filter_kernel(mix, *refs, fresh, inner, chans, lat, width, vox_total, frames):
    total_blocks = (len(refs) - 3) // 2
    gram = refs[2 * total_blocks] if not fresh else None
    mine = refs[:total_blocks]
    other = refs[total_blocks : 2 * total_blocks]
    out, mat_high, mat_low = refs[-3:]
    n = lat * width
    half = mine[0].shape[1]
    hf = half // 2
    vox = lax.axis_index("vox")
    chan = lax.axis_index("chan")
    if fresh:
        a = jnp.concatenate([r[...] for r in mine[:fresh]], axis=0)
        b = jnp.concatenate([r[...] for r in other[:fresh]], axis=0)
        parts = gram_parts(a, b)
    else:
        parts = [(gram[i, 0], gram[i, 1]) for i in range(3)]

    def diag_sum(t):
        r = lax.broadcasted_iota(jnp.int32, (DIAG, DIAG), 0)
        c = lax.broadcasted_iota(jnp.int32, (DIAG, DIAG), 1)
        tiles = [t[i : i + DIAG, i : i + DIAG] for i in range(0, hf, DIAG)]
        return jnp.sum(jnp.where(r == c, functools.reduce(jnp.add, tiles), 0.0))

    factor = frames / (diag_sum(parts[0][0]) + diag_sum(parts[2][0]))
    for i, (real, imag) in enumerate(parts):
        real_high, real_low = split(real)
        imag_high, imag_low = split(imag)
        for ref, re, im in ((mat_high, real_high, imag_high), (mat_low, real_low, imag_low)):
            ref[i, :hf, :hf] = re
            ref[i, hf:, hf:] = re
            ref[i, :hf, hf:] = im
            ref[i, hf:, :hf] = -im

    edge = HALO * width

    def border(blocks, v, away, cut):
        if vox_total > inner:
            return blocks[(inner if v < 0 else inner + 1) * chans + away][cut, :]
        distance = vox ^ jnp.clip(vox + v, 0, vox_total - 1)
        rows = blocks[away][cut, :].astype(F32)
        for d in range(1, inner):
            rows = jnp.where(distance == d, blocks[d * chans + away][cut, :].astype(F32), rows)
        return rows.astype(BF16)

    def column(blocks, away):
        return jnp.concatenate(
            [
                border(blocks, -1, away, slice(n - edge, n)),
                blocks[away][...],
                border(blocks, 1, away, slice(0, edge)),
            ],
            axis=0,
        )

    def any_column(blocks, away):
        if isinstance(away, int):
            return column(blocks, away)
        got = column(blocks, 0).astype(F32)
        for d in range(1, chans):
            got = jnp.where(away == d, column(blocks, d).astype(F32), got)
        return got.astype(BF16)

    lat_all = lat + 2 * HALO
    rows = lat_all * width
    pr = lax.broadcasted_iota(jnp.int32, (lat_all * EDGE, rows), 0)
    pc = lax.broadcasted_iota(jnp.int32, (lat_all * EDGE, rows), 1)
    x_rows = [[column(mine, 0)], [column(other, 0)]]
    for away, start, _ in neighbours(chan, chans, width):
        pick = (pr // EDGE == pc // width) & (pc % width == start + pr % EDGE)
        pick = pick.astype(F32).astype(BF16)
        for which, blocks in enumerate((mine, other)):
            x_rows[which].append(dot(pick, any_column(blocks, away)).astype(BF16))
    xa, xb = (jnp.concatenate(x, axis=0) for x in x_rows)

    def product(z, i, back=False):
        high, low = mat_high[i], mat_low[i]
        if len(z) == 1:
            left, right = [z[0]], [high]
        else:
            left, right = [z[0], z[1], z[0]], [high, high, low]
        axis = 1 if back else 0
        return dot(
            jnp.concatenate(left, axis=1), jnp.concatenate(right, axis=axis), ((1,), (axis,))
        )

    c0, c1, c2, c3 = POLY_COEFFS
    fa, fb = xa.astype(F32), xb.astype(F32)
    first = c3 * factor
    za = first * (product([xa], 0) + product([xb], 1, True)) + c2 * fa
    zb = first * (product([xa], 1) + product([xb], 2)) + c2 * fb
    sa, sb = split(za), split(zb)
    za = factor * (product(sa, 0) + product(sb, 1, True)) + c1 * fa
    zb = factor * (product(sa, 1) + product(sb, 2)) + c1 * fb
    sa, sb = split(za), split(zb)
    za = factor * (product(sa, 0) + product(sb, 1, True)) + c0 * fa
    env = jnp.sqrt(za[:, :hf] * za[:, :hf] + za[:, hf:] * za[:, hf:] + 1e-06)
    eh, el = split(env)
    mh, ml = mix[0], mix[1]
    out[...] = dot(mh, eh) + dot(ml, eh) + dot(mh, el)


def shards(mesh, echo_data, tile_weights, tile_target, tile_offset, tile_count, grid_map, psf_kernel):
    rows, hf = echo_data.shape[2], echo_data.shape[4]
    slots, tile = tile_weights.shape[2], tile_weights.shape[3]
    voxels = grid_map.shape[1]
    chans, vox_total, frms = mesh.shape["chan"], mesh.shape["vox"], mesh.shape["frm"]
    lat = 8
    width = voxels // lat // chans
    n = lat * width
    smem = pl.BlockSpec(memory_space=pltpu.SMEM)
    vmem = pl.BlockSpec(memory_space=pltpu.VMEM)
    hbm = pl.BlockSpec(memory_space=pl.ANY)
    echo = echo_data.reshape(rows, 2, hf)
    seen = (lat + 2 * HALO) * (width + min(chans - 1, 2) * EDGE)
    own, sent, mix = pl.pallas_call(
        functools.partial(das_kernel, chans=chans, lat=lat, vox_total=vox_total),
        out_shape=(
            pltpu.VMEM((n, 2 * hf), F32),
            pltpu.VMEM((chans - 1, n, 2 * hf), F32),
            pltpu.VMEM((2, n, seen), BF16),
        ),
        in_specs=[smem, smem, smem, hbm, hbm, vmem, smem],
        out_specs=(vmem, vmem, vmem),
        scratch_shapes=[
            pltpu.VMEM((rows, 2, hf), BF16),
            pltpu.VMEM((slots, tile, tile), BF16),
            pltpu.VMEM((voxels // tile + 1, rows // tile + 1, tile, tile), F32),
            pltpu.VMEM((voxels, 2 * hf), F32),
            pltpu.SemaphoreType.DMA((CHUNKS + 1,)),
        ],
        compiler_params=pltpu.CompilerParams(vmem_limit_bytes=56 * 2**20),
    )(
        tile_count,
        tile_target.reshape(-1),
        tile_offset.reshape(-1),
        echo,
        tile_weights.reshape(slots, tile, tile),
        grid_map,
        psf_kernel,
    )
    inner = min(vox_total, 4)

    def peer(x, dv, dc):
        pairs = [
            (v * chans + c, (v ^ dv) * chans + (c ^ dc))
            for v in range(vox_total)
            for c in range(chans)
        ]
        return lax.ppermute(x, ("vox", "chan"), pairs)

    for step in range(1, chans):
        own = own + peer(sent[step - 1].astype(jnp.float16), 0, step).astype(F32)
    own = own.astype(BF16)
    crossed = peer(own, inner // 2, 0)
    near = [(dv, dc) for dv in range(inner // 2) for dc in range(chans)]
    first, second = {}, {}
    for i in reversed(range(1, len(near))):
        first[i] = peer(own, *near[i])
    for i in reversed(range(1, len(near))):
        second[i] = peer(crossed, *near[i])
    rest = range(1, len(near))
    mine = [own] + [first[i] for i in rest] + [crossed] + [second[i] for i in rest]

    def to_other(x):
        return lax.ppermute(x, "frm", [(f, f ^ 1) for f in range(frms)])

    groups = inner * chans
    part = groups // 2
    tied = lax.optimization_barrier(tuple(mine[1:part] + mine[part + 1 : part + 3]))
    mine = [mine[0], *tied[: part - 1], mine[part], *tied[part - 1 :], *mine[part + 3 :]]
    other = [to_other(x) for x in mine]

    def gram_of(a, b):
        cost = pl.CostEstimate(
            flops=6 * len(a) * n * (2 * hf) ** 2, bytes_accessed=12 * (2 * hf) ** 2, transcendentals=0
        )
        return pl.pallas_call(
            gram_kernel,
            out_shape=jax.ShapeDtypeStruct((3, 2, hf, hf), F32),
            in_specs=[vmem] * (2 * len(a)),
            out_specs=vmem,
            cost_estimate=cost,
            compiler_params=pltpu.CompilerParams(vmem_limit_bytes=VMEM_LIMIT),
        )(*a, *b)

    fresh, gram = groups, []
    if vox_total > inner:
        fresh, gram = 0, [gram_of(mine, other)]
        away = inner
        while away < vox_total:
            gram = [gram[0] + peer(gram[0], away, 0)]
            away *= 2
        for go in (1, -1):
            pairs = [(v, v + go) for v in range(vox_total) if 0 <= v + go < vox_total]
            mine += [lax.ppermute(x, "vox", pairs) for x in mine[:chans]]
            other += [lax.ppermute(x, "vox", pairs) for x in other[:chans]]
    blocks = len(mine)
    out = pl.pallas_call(
        functools.partial(
            filter_kernel,
            fresh=fresh,
            inner=inner,
            chans=chans,
            lat=lat,
            width=width,
            vox_total=vox_total,
            frames=float(frms * hf),
        ),
        out_shape=jax.ShapeDtypeStruct((n, hf), F32),
        in_specs=[vmem] * (1 + 2 * blocks + len(gram)),
        out_specs=vmem,
        scratch_shapes=[
            pltpu.VMEM((3, 2 * hf, 2 * hf), BF16),
            pltpu.VMEM((3, 2 * hf, 2 * hf), BF16),
        ],
        compiler_params=pltpu.CompilerParams(vmem_limit_bytes=VMEM_LIMIT),
    )(mix, *mine, *other, *gram)
    return out.reshape(lat, width, hf)


def solution(mesh):
    in_specs = (
        P(("groups", "vox"), "chan", None, None, "frm"),
        P("vox", "chan", None, None, None),
        P("vox", "chan", None),
        P("vox", "chan", None),
        P("vox", "chan"),
        P("vox", None),
        P(),
    )
    out_specs = P(("groups", "vox"), "chan", "frm")
    return jax.shard_map(
        functools.partial(shards, mesh),
        mesh=mesh,
        in_specs=in_specs,
        out_specs=out_specs,
        check_vma=False,
    )
```
